256 devices in a mesh: sec: 32 (over x, y, core), mpo: 8 (over z).
Axes of the slice: x: 4, y: 4, z: 8, core: 2. Of those that a mesh axis runs over, the one named last changes fastest.
Arguments:
- wavefunction: float32 [128, 256, 256], P('sec')
- left_env: float32 [40, 128, 256, 256], P('mpo', 'sec')
- right_env: float32 [40, 128, 256, 256], P('mpo', 'sec')
- sector_dims: int32 [128, 2], P('sec'), may hold values from 64 to 256, as said below
- charges: int32 [128, 2], replicated, may hold values from 0 to 15, as said below
- term_class: int32 [40], P('mpo'), may hold values from 0 to 4
Outputs:
- residual: float32 [128, 256, 256], P('sec', 'mpo')
- applied: float32 [128, 256, 256], P('sec', 'mpo')
The draws below stay inside these ranges and needn't reach their ends.
Inputs may be any that keep to these rules, and one draw needn't show every extreme that they name: `charges`: column 0 is a particle-number label n and column 1 a spin label s; every pair with n below 16 and s below 8 is held by exactly one slot; slots k * 4 to (k + 1) * 4 - 1 belong to device k along sec, and 8 n + s minus that device index is the same modulo the number of devices along sec for all slots. `sector_dims`: column 0 is a sector's dimension on the left of the two-site matrix, column 1 on the right; entries of a block outside them are not part of the state.
All inputs are finite; a program needn't handle non-finite values.
Results may differ from the reference program's by a relative error of at most 0.0017.
Values sent between devices are 32-bit elements; how exact they have to be, the bound alone decides.
No kernel may reach another device: no remote copies, remote signals or barrier semaphores. Data moves between devices by JAX's collectives and lax.ppermute only.
A program may use at most 64 MiB of HBM per device.

```python
import math
import jax
import jax.numpy as jnp
from jax import lax

W = 40
BLOCK = 256
SEC_DEV = 4
SECT = 128


def draw_wavefunction(key, part):
    key = jax.random.fold_in(key, 13)
    keys = jax.random.split(key, 5)
    positions = jnp.arange(SECT, dtype=jnp.float32) / max(SECT - 1, 1)
    row_scale = jnp.exp(jax.random.uniform(keys[1], (SECT, BLOCK, 1), minval=-1.15, maxval=1.15))
    col_scale = jnp.exp(jax.random.uniform(keys[2], (SECT, 1, BLOCK), minval=-1.15, maxval=1.15))
    noise = jax.random.normal(keys[0], (SECT, BLOCK, BLOCK))
    sector_scale = 3.0 ** positions
    sector_scale = sector_scale * jnp.exp(jax.random.uniform(keys[4], (SECT,), minval=-0.35, maxval=0.35))
    return (0.2 * noise * row_scale * col_scale * sector_scale[:, None, None]).astype(jnp.float32)


def draw_left_env(key, part):
    key = jax.random.fold_in(key, 14)
    first, second = jax.random.split(key)
    noise = jax.random.normal(first, (W, SECT, BLOCK, BLOCK))
    diagonal = jax.random.uniform(second, (W, SECT, 1, 1), minval=0.5, maxval=1.5)
    positions = jnp.arange(BLOCK)
    identity = (positions[:, None] == positions[None, :]).astype(jnp.float32)
    return (noise / math.sqrt(BLOCK) + diagonal * identity).astype(jnp.float32)


def draw_right_env(key, part):
    key = jax.random.fold_in(key, 15)
    first, second = jax.random.split(key)
    noise = jax.random.normal(first, (W, SECT, BLOCK, BLOCK))
    diagonal = jax.random.uniform(second, (W, SECT, 1, 1), minval=0.5, maxval=1.5)
    positions = jnp.arange(BLOCK)
    identity = (positions[:, None] == positions[None, :]).astype(jnp.float32)
    return ((noise / math.sqrt(BLOCK) + diagonal * identity) / math.sqrt(W)).astype(jnp.float32)


def draw_sector_dims(key, part):
    key = jax.random.fold_in(key, 12)
    first, second = jax.random.split(key)
    values = jax.random.randint(first, (SECT, 2), BLOCK // 4, BLOCK + 1)
    chosen = jax.random.randint(second, (2,), 0, SECT)
    positions = jnp.arange(SECT)
    return jnp.where(positions[:, None] == chosen[None, :], BLOCK, values).astype(jnp.int32)


def draw_charges(key, part):
    key = jax.random.fold_in(key, 11)
    first, second = jax.random.split(key)
    devices_sec = SECT // SEC_DEV
    offset = jax.random.randint(first, (), 0, devices_sec)
    scores = jax.random.randint(second, (devices_sec, SEC_DEV), 0, 1 << 20) * SEC_DEV + jnp.arange(SEC_DEV)[None, :]
    ranking = jnp.argsort(scores, axis=1)
    device_ids = jnp.arange(devices_sec)[:, None]
    labels = ((device_ids + offset) % devices_sec + ranking * devices_sec).reshape(-1)
    return jnp.stack([labels // 8, labels % 8], axis=1).astype(jnp.int32)


def set_ends(array, stream_key, least, largest):
    longest = array.shape.index(max(array.shape))
    spots = []
    for shift in (0, 1):
        where = [jax.random.randint(jax.random.fold_in(stream_key, axis), (), 0, length) for axis, length in enumerate(array.shape)]
        where[longest] = (where[longest] + shift) % array.shape[longest]
        spots.append(tuple(where))
    return array.at[spots[0]].set(least).at[spots[1]].set(largest)


def setup_inputs(seed: int = 0) -> dict:
    key_list = jax.random.split(jax.random.key(seed), 7)
    wavefunction = draw_wavefunction(jax.random.fold_in(key_list[6], 71), 0)
    left_env = draw_left_env(jax.random.fold_in(key_list[6], 71), 0)
    right_env = draw_right_env(jax.random.fold_in(key_list[6], 71), 0)
    sector_dims = draw_sector_dims(jax.random.fold_in(key_list[6], 71), 0)
    charges = draw_charges(jax.random.fold_in(key_list[6], 71), 0)
    term_class = set_ends(jax.random.randint(key_list[5], (W,), 0, 5), jax.random.fold_in(key_list[5], 1), 0, 4).astype(jnp.int32)
    return dict(wavefunction=wavefunction, left_env=left_env, right_env=right_env, sector_dims=sector_dims, charges=charges, term_class=term_class)


number_steps = (0, 1, 1, -1, -1)
spin_steps = (0, 1, -1, 1, -1)


def block_mask(sector_dims, block_size):
    positions = jnp.arange(block_size)
    row_live = positions[None, :, None] < sector_dims[:, 0][:, None, None]
    col_live = positions[None, None, :] < sector_dims[:, 1][:, None, None]
    return (row_live & col_live).astype(jnp.float32)


def class_sources(charges):
    positions = jnp.arange(charges.shape[0])
    sources = []
    present = []
    for charge_kind in range(5):
        matches = (charges[None, :, 0] == charges[:, None, 0] - number_steps[charge_kind]) & (charges[None, :, 1] == charges[:, None, 1] - spin_steps[charge_kind])
        sources.append(jnp.sum(jnp.where(matches, positions[None, :], 0), axis=1))
        present.append(jnp.any(matches, axis=1))
    return jnp.stack(sources), jnp.stack(present)


def apply_hamiltonian(blocks, left_env, right_env, term_class, sources, present, live_mask):
    def add_term(running, inputs):
        left_block, right_block, term_kind = inputs
        gathered = blocks[sources[term_kind]] * present[term_kind].astype(jnp.float32)[:, None, None]
        middle = jnp.einsum("irk,ikc->irc", left_block, gathered, precision=lax.Precision.HIGHEST)
        return running + jnp.einsum("irk,ick->irc", middle, right_block, precision=lax.Precision.HIGHEST), None

    running, unused_out = lax.scan(add_term, jnp.zeros(blocks.shape, jnp.float32), (left_env, right_env, term_class))
    return live_mask * running


def reference(wavefunction, left_env, right_env, sector_dims, charges, term_class):
    live_mask = block_mask(sector_dims, wavefunction.shape[1])
    masked = live_mask * wavefunction
    sources, present = class_sources(charges)
    sigma_one = apply_hamiltonian(masked, left_env, right_env, term_class, sources, present, live_mask)
    quotient = jnp.sum(masked * sigma_one) / jnp.sum(masked * masked)
    residual = sigma_one - quotient * masked
    applied = apply_hamiltonian(residual, left_env, right_env, term_class, sources, present, live_mask)
    return residual, applied
```

```python
import functools
import jax
import jax.numpy as jnp
from jax import lax
from jax.experimental import pallas as pl
from jax.experimental.pallas import tpu as pltpu
from jax.sharding import PartitionSpec as P

number_steps = (0, 1, 1, -1, -1)
spin_steps = (0, 1, -1, 1, -1)
SPINS = 8
RANK, SLOT, SOURCE, LIVE, ROWS, COLS, TERM, PLANE, META = 0, 8, 16, 40, 64, 72, 80, 96, 128


def passed_along(value, axis, by):
    count = lax.axis_size(axis)
    return lax.ppermute(value, axis, [(i, (i + by) % count) for i in range(count)])


def plan_kernel(numbers, charges_ref, dims_ref, term_ref, meta_ref):
    sec_dev = dims_ref.shape[0]
    first = lax.axis_index("sec") * sec_dev
    spin = charges_ref[first, 1]
    residue = charges_ref[first, 0] % (numbers // sec_dev)
    stride = numbers // sec_dev
    for slot in range(sec_dev):
        rank = charges_ref[first + slot, 0] // stride
        meta_ref[RANK + slot] = rank
        meta_ref[SLOT + rank] = slot
        meta_ref[ROWS + rank] = dims_ref[slot, 0]
        meta_ref[COLS + rank] = dims_ref[slot, 1]
    for rank in range(sec_dev):
        number = residue + stride * rank
        for kind in range(5):
            source_number = number - number_steps[kind]
            source_spin = spin - spin_steps[kind]
            inside = (source_number >= 0) & (source_number < numbers) & (source_spin >= 0) & (source_spin < SPINS)
            meta_ref[SOURCE + kind * sec_dev + rank] = jnp.where(inside, source_number // stride, rank)
            meta_ref[LIVE + kind * sec_dev + rank] = jnp.where(inside, 1, 0)
    for term in range(term_ref.shape[0]):
        meta_ref[TERM + term] = term_ref[term]
    meta_ref[PLANE] = lax.axis_index("mpo")


def make_plan(charges, sector_dims, term_class):
    sec_dev = sector_dims.shape[0]
    numbers = charges.shape[0] // SPINS
    return pl.pallas_call(
        functools.partial(plan_kernel, numbers),
        out_shape=jax.ShapeDtypeStruct((META,), jnp.int32),
        in_specs=[pl.BlockSpec(memory_space=pltpu.SMEM)] * 3,
        out_specs=pl.BlockSpec(memory_space=pltpu.SMEM),
    )(charges, sector_dims, term_class)


def live_area(shape, first_row, rows, cols):
    row = lax.broadcasted_iota(jnp.int32, shape, len(shape) - 2) + first_row
    col = lax.broadcasted_iota(jnp.int32, shape, len(shape) - 1)
    return (row < rows) & (col < cols)


def mask_kernel(meta_ref, block_ref, out_ref):
    rank = meta_ref[RANK + pl.program_id(0)]
    block = block_ref[0]
    live = live_area(block.shape, 0, meta_ref[ROWS + rank], meta_ref[COLS + rank])
    out_ref[...] = jnp.where(live, block, 0.0).reshape(out_ref.shape)


def mask_and_sort(meta, wavefunction, planes):
    sec_dev, size, _ = wavefunction.shape
    share = size // planes
    return pl.pallas_call(
        mask_kernel,
        out_shape=jax.ShapeDtypeStruct((planes, sec_dev, share, size), jnp.float32),
        grid_spec=pltpu.PrefetchScalarGridSpec(
            num_scalar_prefetch=1,
            grid=(sec_dev,),
            in_specs=[pl.BlockSpec((1, size, size), lambda i, meta: (i, 0, 0))],
            out_specs=pl.BlockSpec((planes, 1, share, size), lambda i, meta: (0, meta[RANK + i], 0, 0)),
        ),
    )(meta, wavefunction)


def split(value):
    high = value.astype(jnp.bfloat16)
    return high, (value - high.astype(jnp.float32)).astype(jnp.bfloat16)


def product(a, b, contract):
    dims = (((1,), (contract,)), ((), ()))
    dot = functools.partial(lax.dot_general, dimension_numbers=dims, preferred_element_type=jnp.float32)
    return dot(a[0], b[0]) + (dot(a[0], b[1]) + dot(a[1], b[0]))


def terms_kernel(sec_dev, meta_ref, *refs):
    sources, (left_ref, right_ref, out_ref, high_ref, low_ref) = refs[:5], refs[5:]
    rank = pl.program_id(0)
    size = left_ref.shape[-1]
    for kind in range(5):
        live = meta_ref[LIVE + kind * sec_dev + rank] != 0
        high, low = split(jnp.where(live, sources[kind][...].reshape(size, size), 0.0))
        high_ref[kind] = high
        low_ref[kind] = low
    total = None
    for term in range(left_ref.shape[0]):
        kind = meta_ref[TERM + term]
        middle = product(split(left_ref[term, 0]), (high_ref[kind], low_ref[kind]), 0)
        part = product(split(middle), split(right_ref[term, 0]), 1)
        total = part if total is None else total + part
    out_ref[...] = total.reshape(out_ref.shape)


def apply_terms(meta, sources, left_env, right_env):
    planes, sec_dev, share, size = sources[0].shape
    terms = left_env.shape[0]

    def source_spec(kind):
        return pl.BlockSpec(
            (planes, 1, share, size), lambda j, meta: (0, meta[SOURCE + kind * sec_dev + j], 0, 0)
        )

    env_spec = pl.BlockSpec((terms, 1, size, size), lambda j, meta: (0, meta[SLOT + j], 0, 0))
    return pl.pallas_call(
        functools.partial(terms_kernel, sec_dev),
        out_shape=jax.ShapeDtypeStruct((planes, sec_dev, share, size), jnp.float32),
        grid_spec=pltpu.PrefetchScalarGridSpec(
            num_scalar_prefetch=1,
            grid=(sec_dev,),
            in_specs=[source_spec(kind) for kind in range(5)] + [env_spec, env_spec],
            out_specs=pl.BlockSpec((planes, 1, share, size), lambda j, meta: (0, j, 0, 0)),
            scratch_shapes=[pltpu.VMEM((5, size, size), jnp.bfloat16)] * 2,
        ),
        compiler_params=pltpu.CompilerParams(vmem_limit_bytes=40 * 2**20),
        cost_estimate=pl.CostEstimate(
            flops=sec_dev * terms * 12 * size**3, bytes_accessed=4 * sec_dev * size * size * (2 * terms + 6), transcendentals=0
        ),
    )(meta, *sources, left_env, right_env)


def sum_kernel(meta_ref, parts_ref, masked_ref, sigma_ref, sums_ref):
    rank = pl.program_id(0)
    share = sigma_ref.shape[1]
    total = jnp.sum(parts_ref[:, 0], axis=0)
    live = live_area(total.shape, meta_ref[PLANE] * share, meta_ref[ROWS + rank], meta_ref[COLS + rank])
    sigma = jnp.where(live, total, 0.0)
    sigma_ref[0] = sigma
    masked = masked_ref[0, 0]

    @pl.when(rank == 0)
    def _():
        sums_ref[...] = jnp.zeros_like(sums_ref)

    def folded(value):
        return jnp.sum(value.reshape(share // 8, 8, value.shape[1]), axis=0)

    sums_ref[0] += folded(masked * sigma)
    sums_ref[1] += folded(masked * masked)


def sum_parts(meta, parts, masked):
    planes, sec_dev, share, size = parts.shape
    return pl.pallas_call(
        sum_kernel,
        out_shape=(
            jax.ShapeDtypeStruct((sec_dev, share, size), jnp.float32),
            jax.ShapeDtypeStruct((2, 8, size), jnp.float32),
        ),
        grid_spec=pltpu.PrefetchScalarGridSpec(
            num_scalar_prefetch=1,
            grid=(sec_dev,),
            in_specs=[
                pl.BlockSpec((planes, 1, share, size), lambda j, meta: (0, j, 0, 0)),
                pl.BlockSpec((1, 1, share, size), lambda j, meta: (meta[PLANE], j, 0, 0)),
            ],
            out_specs=(
                pl.BlockSpec((1, share, size), lambda j, meta: (j, 0, 0)),
                pl.BlockSpec((2, 8, size), lambda j, meta: (0, 0, 0)),
            ),
        ),
    )(meta, parts, masked)


def final_kernel(meta_ref, parts_ref, sigma_ref, masked_ref, sums_ref, residual_ref, applied_ref):
    rank = pl.program_id(0)
    share = sigma_ref.shape[1]
    quotient = jnp.sum(sums_ref[0], keepdims=True) / jnp.sum(sums_ref[1], keepdims=True)
    total = jnp.sum(parts_ref[:, 0], axis=0)
    live = live_area(total.shape, meta_ref[PLANE] * share, meta_ref[ROWS + rank], meta_ref[COLS + rank])
    sigma = sigma_ref[0]
    residual_ref[0] = sigma - quotient * masked_ref[0, 0]
    applied_ref[0] = jnp.where(live, total, 0.0) - quotient * sigma


def finish(meta, parts, sigma, masked, sums):
    planes, sec_dev, share, size = parts.shape
    out_spec = pl.BlockSpec((1, share, size), lambda j, meta: (meta[SLOT + j], 0, 0))
    return pl.pallas_call(
        final_kernel,
        out_shape=(jax.ShapeDtypeStruct((sec_dev, share, size), jnp.float32),) * 2,
        grid_spec=pltpu.PrefetchScalarGridSpec(
            num_scalar_prefetch=1,
            grid=(sec_dev,),
            in_specs=[
                pl.BlockSpec((planes, 1, share, size), lambda j, meta: (0, j, 0, 0)),
                pl.BlockSpec((1, share, size), lambda j, meta: (j, 0, 0)),
                pl.BlockSpec((1, 1, share, size), lambda j, meta: (meta[PLANE], j, 0, 0)),
                pl.BlockSpec((2, 8, size), lambda j, meta: (0, 0, 0)),
            ],
            out_specs=(out_spec, out_spec),
        ),
    )(meta, parts, sigma, masked, sums)


def from_neighbours(blocks):
    steps = [(SPINS * dn + ds) for dn, ds in zip(number_steps, spin_steps)]
    return [blocks] + [passed_along(blocks, "sec", step) for step in steps[1:]]


def summed_over_devices(value):
    for axis in ("mpo", "sec"):
        count = lax.axis_size(axis)
        step = 1
        while step < count:
            value = value + passed_along(value, axis, step)
            step *= 2
    return value


def local(wavefunction, left_env, right_env, sector_dims, charges, term_class):
    planes = lax.axis_size("mpo")
    meta = make_plan(charges, sector_dims, term_class)
    masked = mask_and_sort(meta, wavefunction, planes)
    first = apply_terms(meta, from_neighbours(masked), left_env, right_env)
    sigma, sums = sum_parts(meta, lax.all_to_all(first, "mpo", 0, 0), masked)
    sigma_full = lax.all_gather(sigma, "mpo", axis=0)
    sums = summed_over_devices(sums)
    second = apply_terms(meta, from_neighbours(sigma_full), left_env, right_env)
    return finish(meta, lax.all_to_all(second, "mpo", 0, 0), sigma, masked, sums)


def solution(mesh):
    placed = (
        P("sec", None, None),
        P("mpo", "sec", None, None),
        P("mpo", "sec", None, None),
        P("sec", None),
        P(),
        P("mpo"),
    )
    return jax.shard_map(
        local,
        mesh=mesh,
        in_specs=placed,
        out_specs=(P("sec", "mpo", None), P("sec", "mpo", None)),
        check_vma=False,
    )
```

```python
import functools
import jax
import jax.numpy as jnp
from jax import lax
from jax.experimental import pallas as pl
from jax.experimental.pallas import tpu as pltpu
from jax.sharding import PartitionSpec as P

number_steps = (0, 1, 1, -1, -1)
spin_steps = (0, 1, -1, 1, -1)
SPINS = 8
GROUPS = ((0, 1, 4), (2, 3))
SOURCE, LIVE, COUNT, ORDER, PICK, META = 0, 32, 64, 72, 104, 136
TERMS_MAX = 16
TILE = 8
SMEM = pl.BlockSpec(memory_space=pltpu.SMEM)
VMEM = pl.BlockSpec(memory_space=pltpu.VMEM)
ANY = pl.BlockSpec(memory_space=pl.ANY)


def distance_of(kind):
    return SPINS * number_steps[kind] + spin_steps[kind]


def passed_along(value, axis, by):
    count = lax.axis_size(axis)
    return lax.ppermute(value, axis, [(i, (i + by) % count) for i in range(count)])


def plan_kernel(sec_dev, charges_ref, term_ref, meta_ref):
    devices = charges_ref.shape[1] // sec_dev
    here = lax.axis_index("sec")
    for kind in range(5):
        sender = lax.rem(here + (devices - distance_of(kind) % devices), devices)
        for slot in range(sec_dev):
            number = charges_ref[0, here * sec_dev + slot] - number_steps[kind]
            spin = charges_ref[1, here * sec_dev + slot] - spin_steps[kind]
            found, live = jnp.int32(0), jnp.int32(0)
            for other in range(sec_dev):
                same = (charges_ref[0, sender * sec_dev + other] == number) & (
                    charges_ref[1, sender * sec_dev + other] == spin
                )
                found = jnp.where(same, other, found)
                live = jnp.where(same, 1, live)
            meta_ref[SOURCE + kind * sec_dev + slot] = found
            meta_ref[LIVE + kind * sec_dev + slot] = live
    counts = [jnp.int32(0) for _ in GROUPS]
    for term in range(term_ref.shape[0]):
        kind = term_ref[term]
        for g, group in enumerate(GROUPS):
            inside, pick = kind == group[0], jnp.int32(0)
            for place, member in enumerate(group[1:], 1):
                inside = inside | (kind == member)
                pick = jnp.where(kind == member, place, pick)
            at = counts[g]
            keep_order = meta_ref[ORDER + g * TERMS_MAX + at]
            keep_pick = meta_ref[PICK + g * TERMS_MAX + at]
            meta_ref[ORDER + g * TERMS_MAX + at] = jnp.where(inside, term, keep_order)
            meta_ref[PICK + g * TERMS_MAX + at] = jnp.where(inside, pick, keep_pick)
            counts[g] = jnp.where(inside, at + 1, at)
    for g in range(len(GROUPS)):
        meta_ref[COUNT + g] = counts[g]


def make_plan(charges, term_class, sec_dev):
    return pl.pallas_call(
        functools.partial(plan_kernel, sec_dev),
        out_shape=jax.ShapeDtypeStruct((META,), jnp.int32),
        in_specs=[SMEM] * 2,
        out_specs=SMEM,
    )(charges.T, term_class)


def live_area(shape, first_row, rows, cols):
    row = lax.broadcasted_iota(jnp.int32, shape, len(shape) - 2) + first_row
    col = lax.broadcasted_iota(jnp.int32, shape, len(shape) - 1)
    return (row < rows) & (col < cols)


def mask_kernel(dims_ref, block_ref, out_ref, own_ref):
    planes = out_ref.shape[0]
    sec_dev, size, _ = block_ref.shape
    share = size // planes
    for slot in range(sec_dev):
        live = live_area((size, size), 0, dims_ref[0, slot], dims_ref[1, slot])
        masked = jnp.where(live, block_ref[slot], 0.0).reshape(planes, share, size)
        out_ref[:, slot * share : (slot + 1) * share, :] = masked
    own_ref[...] = out_ref[lax.axis_index("mpo")]


def mask_blocks(sector_dims, wavefunction, planes):
    sec_dev, size, _ = wavefunction.shape
    rows = sec_dev * size // planes
    return pl.pallas_call(
        mask_kernel,
        out_shape=(
            jax.ShapeDtypeStruct((planes, rows, size), jnp.float32),
            jax.ShapeDtypeStruct((rows, size), jnp.float32),
        ),
        in_specs=[SMEM, VMEM],
        out_specs=(VMEM, VMEM),
    )(sector_dims.T, wavefunction)


def split(value):
    high = value.astype(jnp.bfloat16)
    return high, (value - high.astype(jnp.float32)).astype(jnp.bfloat16)


def product(a, b, contract):
    dims = (((1,), (contract,)), ((), ()))
    dot = functools.partial(lax.dot_general, dimension_numbers=dims, preferred_element_type=jnp.float32)
    return dot(a[0], b[0]) + (dot(a[0], b[1]) + dot(a[1], b[0]))


def terms_kernel(group, sec_dev, meta_ref, *refs):
    kinds = GROUPS[group]
    inputs, (out_ref, high_ref, low_ref, left_buf, right_buf, sems) = refs[:-6], refs[-6:]
    left_ref, right_ref = inputs[:2]
    count = meta_ref[COUNT + group]
    size = left_ref.shape[-1]
    share = size // out_ref.shape[0]
    rows = sec_dev * share

    def copies(at):
        term = meta_ref[ORDER + group * TERMS_MAX + at]
        return (
            pltpu.make_async_copy(left_ref.at[term], left_buf.at[at], sems.at[0, at]),
            pltpu.make_async_copy(right_ref.at[term], right_buf.at[at], sems.at[1, at]),
        )

    @pl.loop(0, count)
    def _(at):
        for copy in copies(at):
            copy.start()

    for place, kind in enumerate(kinds):
        for slot in range(sec_dev):
            found = pl.multiple_of(meta_ref[SOURCE + kind * sec_dev + slot] * share, share)
            live = meta_ref[LIVE + kind * sec_dev + slot] != 0
            if group == 0:
                block = inputs[2 + place][:, pl.ds(found, share), :]
            else:
                block = inputs[2][:, place, pl.ds(found, share), :]
            high, low = split(jnp.where(live, block.reshape(size, size), 0.0))
            high_ref[place, slot] = high
            low_ref[place, slot] = low
    if group == 0:
        out_ref[...] = jnp.zeros_like(out_ref)
    else:
        out_ref[:, :rows, :] = inputs[3][...]

    @pl.loop(0, count)
    def _(at):
        for copy in copies(at):
            copy.wait()
        place = meta_ref[PICK + group * TERMS_MAX + at]
        for slot in range(sec_dev):
            source = high_ref[place, slot], low_ref[place, slot]
            middle = product(split(left_buf[at, slot]), source, 0)
            part = product(split(middle), split(right_buf[at, slot]), 1)
            out_ref[:, slot * share : (slot + 1) * share, :] += part.reshape(-1, share, size)

    if group == 1 and out_ref.shape[1] > rows:
        sums = inputs[4][...] + inputs[5][...]
        out_ref[:, rows:, :] = jnp.broadcast_to(sums[None], (out_ref.shape[0],) + sums.shape)


def apply_terms(group, meta, sources, left_env, right_env, so_far=(), sums=()):
    terms, sec_dev, size, _ = left_env.shape
    planes = sources[0].shape[0]
    rows = sec_dev * size // planes + (TILE if sums else 0)
    others = [*sources, *so_far, *sums]
    kinds = len(GROUPS[group])
    return pl.pallas_call(
        functools.partial(terms_kernel, group, sec_dev),
        out_shape=jax.ShapeDtypeStruct((planes, rows, size), jnp.float32),
        in_specs=[SMEM, ANY, ANY] + [VMEM] * len(others),
        out_specs=VMEM,
        scratch_shapes=[
            pltpu.VMEM((kinds, sec_dev, size, size), jnp.bfloat16),
            pltpu.VMEM((kinds, sec_dev, size, size), jnp.bfloat16),
            pltpu.VMEM((terms, sec_dev, size, size), jnp.float32),
            pltpu.VMEM((terms, sec_dev, size, size), jnp.float32),
            pltpu.SemaphoreType.DMA((2, terms)),
        ],
        compiler_params=pltpu.CompilerParams(vmem_limit_bytes=36 * 2**20),
        cost_estimate=pl.CostEstimate(
            flops=sec_dev * terms * 6 * size**3, bytes_accessed=4 * sec_dev * size * size * (terms + 4), transcendentals=0
        ),
    )(meta, left_env, right_env, *others)


def folded(value):
    while value.shape[0] > TILE:
        half = value.shape[0] // 2
        value = value[:half] + value[half:]
    return value


def sum_kernel(dims_ref, parts_ref, masked_ref, sigma_ref, payload_ref):
    planes, rows, size = parts_ref.shape
    sec_dev = dims_ref.shape[1]
    share = rows // sec_dev
    first_row = lax.axis_index("mpo") * share
    products, squares = [], []
    for slot in range(sec_dev):
        here = slice(slot * share, (slot + 1) * share)
        total = jnp.sum(parts_ref[:, here, :], axis=0)
        live = live_area(total.shape, first_row, dims_ref[0, slot], dims_ref[1, slot])
        sigma = jnp.where(live, total, 0.0)
        masked = masked_ref[here, :]
        sigma_ref[here, :] = sigma
        payload_ref[:, here, :] = jnp.broadcast_to(sigma[None], (planes, share, size))
        products.append(folded(masked * sigma))
        squares.append(folded(masked * masked))
    half = size // 2
    both = [sum(x[:, :half] + x[:, half:] for x in values) for values in (products, squares)]
    sums = jnp.concatenate(both, axis=1)
    payload_ref[:, rows:, :] = jnp.broadcast_to(sums[None], (planes, TILE, size))


def sum_parts(sector_dims, parts, masked):
    planes, rows, size = parts.shape
    return pl.pallas_call(
        sum_kernel,
        out_shape=(
            jax.ShapeDtypeStruct((rows, size), jnp.float32),
            jax.ShapeDtypeStruct((planes, rows + TILE, size), jnp.float32),
        ),
        in_specs=[SMEM, VMEM, VMEM],
        out_specs=(VMEM, VMEM),
    )(sector_dims.T, parts, masked)


def tile_kernel(one_ref, other_ref, sums_ref):
    rows = one_ref.shape[1] - TILE
    sums_ref[...] = jnp.sum(one_ref[:, rows:, :] + other_ref[:, rows:, :], axis=0)


def add_tiles(one, other):
    planes, rows, size = one.shape
    return pl.pallas_call(
        tile_kernel,
        out_shape=jax.ShapeDtypeStruct((TILE, size), jnp.float32),
        in_specs=[VMEM, VMEM],
        out_specs=VMEM,
    )(one, other)


def final_kernel(dims_ref, parts_ref, sigma_ref, masked_ref, residual_ref, applied_ref):
    sec_dev, share, size = residual_ref.shape
    first_row = lax.axis_index("mpo") * share
    sums = jnp.sum(parts_ref[:, sec_dev * share :, :], axis=0)
    half = size // 2
    quotient = jnp.sum(sums[:, :half], keepdims=True) / jnp.sum(sums[:, half:], keepdims=True)
    for slot in range(sec_dev):
        here = slice(slot * share, (slot + 1) * share)
        total = jnp.sum(parts_ref[:, here, :], axis=0)
        live = live_area(total.shape, first_row, dims_ref[0, slot], dims_ref[1, slot])
        sigma = sigma_ref[here, :]
        residual_ref[slot] = sigma - quotient * masked_ref[here, :]
        applied_ref[slot] = jnp.where(live, total, 0.0) - quotient * sigma


def finish(sector_dims, parts, sigma, masked):
    sec_dev = sector_dims.shape[0]
    rows, size = sigma.shape
    return pl.pallas_call(
        final_kernel,
        out_shape=(jax.ShapeDtypeStruct((sec_dev, rows // sec_dev, size), jnp.float32),) * 2,
        in_specs=[SMEM, VMEM, VMEM, VMEM],
        out_specs=(VMEM, VMEM),
    )(sector_dims.T, parts, sigma, masked)


def spread(sums):
    devices, planes = lax.axis_size("sec"), lax.axis_size("mpo")
    step = devices // planes
    return tuple(
        lax.ppermute(
            sums,
            ("sec", "mpo"),
            [
                (((i + step * m + more) % devices) * planes + m, i * planes + m)
                for i in range(devices)
                for m in range(planes)
            ],
        )
        for more in (0, 1)
    )


def gathered(share):
    pair = jnp.stack([passed_along(share, "sec", distance_of(kind)) for kind in GROUPS[1]])
    return pair, lax.all_gather(pair, "mpo", axis=0)


def direct(blocks):
    return [blocks] + [passed_along(blocks, "sec", distance_of(kind)) for kind in GROUPS[0][1:]]


def local(wavefunction, left_env, right_env, sector_dims, charges, term_class):
    planes = lax.axis_size("mpo")
    sec_dev = wavefunction.shape[0]
    masked, masked_share = mask_blocks(sector_dims, wavefunction, planes)
    pair, shares = gathered(masked_share)
    meta = make_plan(charges, term_class, sec_dev)
    first = apply_terms(0, meta, direct(masked), left_env, right_env)
    first = apply_terms(1, meta, [shares], left_env, right_env, [first])
    sigma, payload = sum_parts(sector_dims, lax.all_to_all(first, "mpo", 0, 0), masked_share)
    pair, shares = gathered(sigma)
    payload, pair = lax.optimization_barrier((payload, pair))
    sources = direct(lax.all_to_all(payload, "mpo", 0, 0))
    sums = spread(add_tiles(sources[1], sources[2]))
    second = apply_terms(0, meta, sources, left_env, right_env)
    second = apply_terms(1, meta, [shares], left_env, right_env, [second], sums)
    return finish(sector_dims, lax.all_to_all(second, "mpo", 0, 0), sigma, masked_share)


def solution(mesh):
    placed = (
        P("sec", None, None),
        P("mpo", "sec", None, None),
        P("mpo", "sec", None, None),
        P("sec", None),
        P(),
        P("mpo"),
    )
    return jax.shard_map(
        local,
        mesh=mesh,
        in_specs=placed,
        out_specs=(P("sec", "mpo", None), P("sec", "mpo", None)),
        check_vma=False,
    )
```

```python
import functools
import jax
import jax.numpy as jnp
from jax import lax
from jax.experimental import pallas as pl
from jax.experimental.pallas import tpu as pltpu
from jax.sharding import PartitionSpec as P

number_steps = (0, 1, 1, -1, -1)
spin_steps = (0, 1, -1, 1, -1)
SPINS = 8
GROUPS = ((0, 2, 3), (1, 4), (0, 2, 3, 1, 4))
SOURCE, LIVE, COUNT, ORDER, PICK, USED, META = 0, 32, 64, 72, 104, 136, 144
TERMS_MAX = 8
TILE = 8
AHEAD = 2
SMEM = pl.BlockSpec(memory_space=pltpu.SMEM)
VMEM = pl.BlockSpec(memory_space=pltpu.VMEM)
ANY = pl.BlockSpec(memory_space=pl.ANY)
KERNEL_VMEM = 50 * 2**20
SMALL = pltpu.CompilerParams(vmem_limit_bytes=8 * 2**20)


def distance_of(kind):
    return SPINS * number_steps[kind] + spin_steps[kind]


def passed_along(value, axis, by):
    count = lax.axis_size(axis)
    return lax.ppermute(value, axis, [(i, (i + by) % count) for i in range(count)])


def plan_kernel(sec_dev, charges_ref, term_ref, meta_ref):
    devices = charges_ref.shape[1] // sec_dev
    here = lax.axis_index("sec")
    for kind in range(5):
        sender = lax.rem(here + (devices - distance_of(kind) % devices), devices)
        for slot in range(sec_dev):
            number = charges_ref[0, here * sec_dev + slot] - number_steps[kind]
            spin = charges_ref[1, here * sec_dev + slot] - spin_steps[kind]
            found, live = jnp.int32(0), jnp.int32(0)
            for other in range(sec_dev):
                same = (charges_ref[0, sender * sec_dev + other] == number) & (
                    charges_ref[1, sender * sec_dev + other] == spin
                )
                found = jnp.where(same, other, found)
                live = jnp.where(same, 1, live)
            meta_ref[SOURCE + kind * sec_dev + slot] = found
            meta_ref[LIVE + kind * sec_dev + slot] = live
    counts = [jnp.int32(0) for _ in GROUPS]
    for kind in range(5):
        used = jnp.int32(0)
        for term in range(term_ref.shape[0]):
            used = jnp.where(term_ref[term] == kind, 1, used)
        meta_ref[USED + kind] = used
    for term in range(term_ref.shape[0]):
        kind = term_ref[term]
        for g, group in enumerate(GROUPS):
            inside, pick = kind == group[0], jnp.int32(0)
            for place, member in enumerate(group[1:], 1):
                inside = inside | (kind == member)
                pick = jnp.where(kind == member, place, pick)
            at = counts[g]
            keep_order = meta_ref[ORDER + g * TERMS_MAX + at]
            keep_pick = meta_ref[PICK + g * TERMS_MAX + at]
            meta_ref[ORDER + g * TERMS_MAX + at] = jnp.where(inside, term, keep_order)
            meta_ref[PICK + g * TERMS_MAX + at] = jnp.where(inside, pick, keep_pick)
            counts[g] = jnp.where(inside, at + 1, at)
    for g in range(len(GROUPS)):
        meta_ref[COUNT + g] = counts[g]


def make_plan(charges, term_class, sec_dev):
    return pl.pallas_call(
        functools.partial(plan_kernel, sec_dev),
        out_shape=jax.ShapeDtypeStruct((META,), jnp.int32),
        in_specs=[SMEM] * 2,
        out_specs=SMEM,
        compiler_params=SMALL,
    )(charges.T, term_class)


def live_area(shape, first_row, rows, cols):
    row = lax.broadcasted_iota(jnp.int32, shape, len(shape) - 2) + first_row
    col = lax.broadcasted_iota(jnp.int32, shape, len(shape) - 1)
    return (row < rows) & (col < cols)


def mask_kernel(dims_ref, block_ref, out_ref, low_ref, own_ref, own_high_ref):
    planes = out_ref.shape[0]
    sec_dev, size, _ = block_ref.shape
    share = size // planes
    direct_rows = low_ref.shape[1]
    for slot in range(sec_dev):
        live = live_area((size, size), 0, dims_ref[0, slot], dims_ref[1, slot])
        masked = jnp.where(live, block_ref[slot], 0.0).reshape(planes, share, size)
        here = slice(slot * share, (slot + 1) * share)
        out_ref[:, here, :] = masked
        if (slot + 1) * share <= direct_rows:
            low_ref[:, here, :] = masked
    own = out_ref[lax.axis_index("mpo")]
    own_ref[...] = own
    own_high_ref[...] = own[direct_rows:]


def mask_blocks(sector_dims, wavefunction, planes):
    sec_dev, size, _ = wavefunction.shape
    rows = sec_dev * size // planes
    shapes = ((planes, rows, size), (planes, rows // 2, size), (rows, size), (rows - rows // 2, size))
    return pl.pallas_call(
        mask_kernel,
        out_shape=[jax.ShapeDtypeStruct(shape, jnp.float32) for shape in shapes],
        in_specs=[SMEM, VMEM],
        out_specs=[VMEM] * 4,
        compiler_params=SMALL,
    )(sector_dims.T, wavefunction)


def split(value):
    high = value.astype(jnp.bfloat16)
    return high, (value - high.astype(jnp.float32)).astype(jnp.bfloat16)


def product(a, b, contract):
    dims = (((1,), (contract,)), ((), ()))
    dot = functools.partial(lax.dot_general, dimension_numbers=dims, preferred_element_type=jnp.float32)
    return dot(a[0], b[0]) + (dot(a[0], b[1]) + dot(a[1], b[0]))


def folded(value):
    while value.shape[0] > TILE:
        half = value.shape[0] // 2
        value = value[:half] + value[half:]
    return value


def halved(one, other):
    half = one.shape[1] // 2
    return jnp.concatenate([x[:, :half] + x[:, half:] for x in (one, other)], axis=1)


def terms_kernel(group, sec_dev, places, turned, last, added, meta_ref, *refs):
    operands = 1 + max(at for held, _ in places for at in held) + any(part is not None for _, part in places)
    left_ref, right_ref = refs[:2]
    sources, refs = refs[2 : 2 + operands], refs[2 + operands :]
    *refs, high_ref, low_ref, left_buf, right_buf, sems = refs
    count = meta_ref[COUNT + group]
    kinds, _, size, _ = high_ref.shape

    def env_copies(at):
        term = meta_ref[ORDER + group * TERMS_MAX + at]
        return (
            pltpu.make_async_copy(left_ref.at[term], left_buf.at[at], sems.at[0, at]),
            pltpu.make_async_copy(right_ref.at[term], right_buf.at[at], sems.at[1, at]),
        )

    @pl.loop(0, count)
    def _(at):
        for copy in env_copies(at):
            copy.start()

    others, refs = refs[:added], refs[added:]
    *pieces, total_ref = refs
    total_ref[...] = others[0][...] if added > 1 else jnp.zeros_like(total_ref)
    planes, rows, _ = total_ref.shape
    share = rows // sec_dev
    plane = lax.axis_index("mpo")

    def prepare(k, kind, held, part):
        groups = [sources[at].at[i] for at in held for i in range(sources[at].shape[0])]
        direct = sec_dev if part is None else groups[0].shape[0] // share if held else 0
        for slot in range(sec_dev):
            found = meta_ref[SOURCE + kind * sec_dev + slot]
            live = meta_ref[LIVE + kind * sec_dev + slot] != 0
            first = pl.ds(pl.multiple_of(jnp.minimum(found, max(direct, 1) - 1) * share, share), share)
            second = pl.ds(pl.multiple_of(jnp.maximum(found - direct, 0) * share, share), share)
            for r in range(planes):
                to = lax.rem(plane + (planes + AHEAD - r), planes) if turned else r
                if part is None:
                    block = groups[r][first, :]
                else:
                    block = sources[-1][to, part, second, :]
                    if direct:
                        block = jnp.where(found < direct, groups[r][first, :], block)
                high, low = split(jnp.where(live, block, 0.0))
                to = pl.ds(pl.multiple_of(to * share, share), share)
                high_ref[k, slot, to, :] = high
                low_ref[k, slot, to, :] = low

    for k, (held, part) in enumerate(places):
        kind = GROUPS[group][k]
        pl.when(meta_ref[USED + kind] != 0)(functools.partial(prepare, k, kind, held, part))

    @pl.loop(0, count)
    def _(at):
        for copy in env_copies(at):
            copy.wait()
        k = meta_ref[PICK + group * TERMS_MAX + at]
        for slot in range(sec_dev):
            middle = product(split(left_buf[at, slot]), (high_ref[k, slot], low_ref[k, slot]), 0)
            part = product(split(middle), split(right_buf[at, slot]), 1)
            total_ref[:, slot * share : (slot + 1) * share, :] += part.reshape(-1, share, size)

    if last:
        own_ref, up_ref, down_ref, far_ref, two_up_ref, two_down_ref = pieces
        if added == 1:
            sums = others[0][...]
        else:
            masked_ref = others[1]
            products = [folded(total_ref[r] * masked_ref[r]) for r in range(planes)]
            own = masked_ref[plane]
            sums = halved(sum(products), folded(own * own))
        outs = (
            (own_ref, 0), (up_ref.at[0], 1), (up_ref.at[1], 3), (down_ref.at[0], -1), (down_ref.at[1], -3),
            (far_ref, 4), (two_up_ref, 2), (two_down_ref, -2),
        )
        for out_ref, away in outs:
            out_ref[:rows, :] = total_ref[lax.rem(plane + (planes + away), planes)]
            out_ref[rows:, :] = sums


def apply_terms(group, meta, operands, places, turned, envs, others=()):
    terms, sec_dev, size, _ = envs[0].shape
    planes = sum(operands[at].shape[0] for at in places[0][0])
    rows = sec_dev * size // planes
    kinds = len(GROUPS[group])
    last = bool(others)
    total = (planes, rows, size)
    scratch = [pltpu.VMEM((kinds, sec_dev, size, size), jnp.bfloat16)] * 2
    scratch += [pltpu.VMEM(envs[0].shape, jnp.float32)] * 2
    scratch += [pltpu.SemaphoreType.DMA((2, terms))]
    if last:
        piece = (rows + TILE, size)
        outs = [piece, (2, *piece), (2, *piece), piece, piece, piece]
        scratch = [pltpu.VMEM(total, jnp.float32)] + scratch
    else:
        outs = [total]
    got = pl.pallas_call(
        functools.partial(terms_kernel, group, sec_dev, places, turned, last, len(others)),
        out_shape=[jax.ShapeDtypeStruct(shape, jnp.float32) for shape in outs],
        in_specs=[SMEM, ANY, ANY] + [VMEM] * (len(operands) + len(others)),
        out_specs=[VMEM] * len(outs),
        scratch_shapes=scratch,
        compiler_params=pltpu.CompilerParams(vmem_limit_bytes=KERNEL_VMEM),
        cost_estimate=pl.CostEstimate(
            flops=sec_dev * terms * 6 * size**3, bytes_accessed=4 * sec_dev * size * size * (terms + 4), transcendentals=0
        ),
    )(meta, *envs, *operands, *others)
    return got if last else got[0]


def middle_kernel(two_up_ref, two_down_ref, up_ref, down_ref, far_ref, sum_up_ref, sum_down_ref):
    sum_up_ref[...] = two_up_ref[...] + up_ref[1]
    sum_down_ref[...] = two_down_ref[...] + (down_ref[1] + far_ref[...])


def reduce_over_planes(pieces):
    own, up, down, far, two_up, two_down = pieces
    up = passed_along(up, "mpo", 1)
    down = passed_along(down, "mpo", -1)
    far = passed_along(far, "mpo", -2)
    shape = jax.ShapeDtypeStruct(own.shape, jnp.float32)
    sum_up, sum_down = pl.pallas_call(
        middle_kernel, out_shape=(shape, shape), in_specs=[VMEM] * 5, out_specs=(VMEM, VMEM), compiler_params=SMALL
    )(two_up, two_down, up, down, far)
    return own, up, down, passed_along(sum_up, "mpo", 2), passed_along(sum_down, "mpo", -2)


def summed(refs, here):
    own_ref, up_ref, down_ref, two_up_ref, two_down_ref = refs
    near = own_ref[here, :] + (up_ref[0, here, :] + down_ref[0, here, :])
    return near + (two_up_ref[here, :] + two_down_ref[here, :])


def sum_kernel(dims_ref, *refs):
    *parts, sigma_ref, payload_ref = refs
    rows, _ = sigma_ref.shape
    sec_dev = dims_ref.shape[1]
    share = rows // sec_dev
    first_row = lax.axis_index("mpo") * share
    for slot in range(sec_dev):
        here = slice(slot * share, (slot + 1) * share)
        total = summed(parts, here)
        live = live_area(total.shape, first_row, dims_ref[0, slot], dims_ref[1, slot])
        sigma = jnp.where(live, total, 0.0)
        sigma_ref[here, :] = sigma
        payload_ref[here, :] = sigma
    payload_ref[rows:, :] = summed(parts, slice(rows, rows + TILE))


def sum_parts(sector_dims, parts):
    rows, size = parts[0].shape
    return pl.pallas_call(
        sum_kernel,
        out_shape=(
            jax.ShapeDtypeStruct((rows - TILE, size), jnp.float32),
            jax.ShapeDtypeStruct((rows, size), jnp.float32),
        ),
        in_specs=[SMEM] + [VMEM] * 5,
        out_specs=(VMEM, VMEM),
        compiler_params=SMALL,
    )(sector_dims.T, *parts)


def pair_kernel(one_ref, other_ref, pair_ref, sums_ref):
    rows = pair_ref.shape[1]
    pair_ref[0] = one_ref[:rows, :]
    pair_ref[1] = other_ref[:rows, :]
    sums_ref[...] = one_ref[rows:, :] + other_ref[rows:, :]


def make_pair(one, other):
    rows, size = one.shape
    return pl.pallas_call(
        pair_kernel,
        out_shape=(
            jax.ShapeDtypeStruct((2, rows - TILE, size), jnp.float32),
            jax.ShapeDtypeStruct((TILE, size), jnp.float32),
        ),
        in_specs=[VMEM] * 2,
        out_specs=(VMEM, VMEM),
        compiler_params=SMALL,
    )(one, other)


def assemble_kernel(*refs):
    *pieces, full_ref = refs
    for r, piece_ref in enumerate(pieces):
        full_ref[r] = piece_ref[...]


def assemble(pieces):
    return pl.pallas_call(
        assemble_kernel,
        out_shape=jax.ShapeDtypeStruct((len(pieces), *pieces[0].shape), jnp.float32),
        in_specs=[VMEM] * len(pieces),
        out_specs=VMEM,
        compiler_params=SMALL,
    )(*pieces)


def final_kernel(dims_ref, *refs):
    parts, (sigma_ref, masked_ref, residual_ref, applied_ref) = refs[:5], refs[5:]
    sec_dev, share, size = residual_ref.shape
    first_row = lax.axis_index("mpo") * share
    sums = summed(parts, slice(sec_dev * share, sec_dev * share + TILE))
    half = size // 2
    quotient = jnp.sum(sums[:, :half], keepdims=True) / jnp.sum(sums[:, half:], keepdims=True)
    for slot in range(sec_dev):
        here = slice(slot * share, (slot + 1) * share)
        total = summed(parts, here)
        live = live_area(total.shape, first_row, dims_ref[0, slot], dims_ref[1, slot])
        sigma = sigma_ref[here, :]
        residual_ref[slot] = sigma - quotient * masked_ref[here, :]
        applied_ref[slot] = jnp.where(live, total, 0.0) - quotient * sigma


def finish(sector_dims, parts, sigma, masked):
    sec_dev = sector_dims.shape[0]
    rows, size = masked.shape
    return pl.pallas_call(
        final_kernel,
        out_shape=(jax.ShapeDtypeStruct((sec_dev, rows // sec_dev, size), jnp.float32),) * 2,
        in_specs=[SMEM] + [VMEM] * 7,
        out_specs=(VMEM, VMEM),
        compiler_params=SMALL,
    )(sector_dims.T, *parts, sigma, masked)


def spread(sums):
    devices, planes = lax.axis_size("sec"), lax.axis_size("mpo")
    step = devices // planes
    return [
        lax.ppermute(
            sums,
            ("sec", "mpo"),
            [(((i + step * m + more) % devices) * planes + m, i * planes + m) for i in range(devices) for m in range(planes)],
        )
        for more in range(step // 2)
    ]


def sent(blocks, kinds):
    return [passed_along(blocks, "sec", distance_of(kind)) for kind in kinds]


def local(wavefunction, left_env, right_env, sector_dims, charges, term_class):
    planes = lax.axis_size("mpo")
    sec_dev = wavefunction.shape[0]
    envs = (left_env, right_env)
    whole_kinds, part_kinds = GROUPS[0][1:], GROUPS[1]
    masked, low, masked_share, high_share = mask_blocks(sector_dims, wavefunction, planes)
    shares = lax.all_gather(jnp.stack(sent(high_share, part_kinds)), "mpo", axis=0)
    meta = make_plan(charges, term_class, sec_dev)
    whole, part = sent(masked, whole_kinds), sent(low, part_kinds)
    whole_places = (((0,), None), ((1,), None), ((2,), None))
    first = apply_terms(0, meta, [masked, *whole], whole_places, False, envs)
    pieces = apply_terms(1, meta, [*part, shares], (((0,), 0), ((1,), 1)), False, envs, [first, masked])
    sigma, payload = sum_parts(sector_dims, reduce_over_planes(pieces))

    pair, sums = make_pair(*sent(payload, part_kinds))
    one, back_one = passed_along(sigma, "mpo", 1), passed_along(sigma, "mpo", -1)
    two, back_two = passed_along(sigma, "mpo", 2), passed_along(sigma, "mpo", -2)
    one, back_one, two, pair = lax.optimization_barrier((one, back_one, two, pair))
    shares = lax.all_gather(pair, "mpo", axis=0)
    three, back_three = passed_along(one, "mpo", 2), passed_along(back_one, "mpo", -2)
    four = passed_along(two, "mpo", 2)
    full = assemble([back_two, back_one, sigma, one, two, three, four, back_three])
    whole = sent(full, whole_kinds)
    full, sums = lax.optimization_barrier((full, sums))
    some, others = spread(sums)

    places = (*whole_places, ((), 0), ((), 1))
    pieces = apply_terms(2, meta, [full, *whole, shares], places, True, envs, [some + others])
    return finish(sector_dims, reduce_over_planes(pieces), sigma, masked_share)


def solution(mesh):
    placed = (
        P("sec", None, None),
        P("mpo", "sec", None, None),
        P("mpo", "sec", None, None),
        P("sec", None),
        P(),
        P("mpo"),
    )
    return jax.shard_map(
        local,
        mesh=mesh,
        in_specs=placed,
        out_specs=(P("sec", "mpo", None), P("sec", "mpo", None)),
        check_vma=False,
    )
```

```python
import functools
import jax
import jax.numpy as jnp
from jax import lax
from jax.experimental import pallas as pl
from jax.experimental.pallas import tpu as pltpu
from jax.sharding import PartitionSpec as P

number_steps = (0, 1, 1, -1, -1)
spin_steps = (0, 1, -1, 1, -1)
SPINS = 8
GROUPS = ((0, 2, 3), (1, 4), (0, 2, 3, 1, 4))
SOURCE, LIVE, COUNT, ORDER, PICK, USED, META = 0, 32, 64, 72, 104, 136, 144
TERMS_MAX = 8
TILE = 8
AHEAD = 1
SMEM = pl.BlockSpec(memory_space=pltpu.SMEM)
VMEM = pl.BlockSpec(memory_space=pltpu.VMEM)
ANY = pl.BlockSpec(memory_space=pl.ANY)
KERNEL_VMEM = 50 * 2**20
SMALL = pltpu.CompilerParams(vmem_limit_bytes=8 * 2**20)


def distance_of(kind):
    return SPINS * number_steps[kind] + spin_steps[kind]


def passed_along(value, axis, by):
    count = lax.axis_size(axis)
    return lax.ppermute(value, axis, [(i, (i + by) % count) for i in range(count)])


def plan_kernel(sec_dev, charges_ref, term_ref, meta_ref):
    devices = charges_ref.shape[1] // sec_dev
    here = lax.axis_index("sec")
    for kind in range(5):
        sender = lax.rem(here + (devices - distance_of(kind) % devices), devices)
        for slot in range(sec_dev):
            number = charges_ref[0, here * sec_dev + slot] - number_steps[kind]
            spin = charges_ref[1, here * sec_dev + slot] - spin_steps[kind]
            found, live = jnp.int32(0), jnp.int32(0)
            for other in range(sec_dev):
                same = (charges_ref[0, sender * sec_dev + other] == number) & (
                    charges_ref[1, sender * sec_dev + other] == spin
                )
                found = jnp.where(same, other, found)
                live = jnp.where(same, 1, live)
            meta_ref[SOURCE + kind * sec_dev + slot] = found
            meta_ref[LIVE + kind * sec_dev + slot] = live
    counts = [jnp.int32(0) for _ in GROUPS]
    for kind in range(5):
        used = jnp.int32(0)
        for term in range(term_ref.shape[0]):
            used = jnp.where(term_ref[term] == kind, 1, used)
        meta_ref[USED + kind] = used
    for term in range(term_ref.shape[0]):
        kind = term_ref[term]
        for g, group in enumerate(GROUPS):
            inside, pick = kind == group[0], jnp.int32(0)
            for place, member in enumerate(group[1:], 1):
                inside = inside | (kind == member)
                pick = jnp.where(kind == member, place, pick)
            at = counts[g]
            keep_order = meta_ref[ORDER + g * TERMS_MAX + at]
            keep_pick = meta_ref[PICK + g * TERMS_MAX + at]
            meta_ref[ORDER + g * TERMS_MAX + at] = jnp.where(inside, term, keep_order)
            meta_ref[PICK + g * TERMS_MAX + at] = jnp.where(inside, pick, keep_pick)
            counts[g] = jnp.where(inside, at + 1, at)
    for g in range(len(GROUPS)):
        meta_ref[COUNT + g] = counts[g]


def make_plan(charges, term_class, sec_dev):
    return pl.pallas_call(
        functools.partial(plan_kernel, sec_dev),
        out_shape=jax.ShapeDtypeStruct((META,), jnp.int32),
        in_specs=[SMEM] * 2,
        out_specs=SMEM,
        compiler_params=SMALL,
    )(charges.T, term_class)


def live_area(shape, first_row, rows, cols):
    row = lax.broadcasted_iota(jnp.int32, shape, len(shape) - 2) + first_row
    col = lax.broadcasted_iota(jnp.int32, shape, len(shape) - 1)
    return (row < rows) & (col < cols)


def mask_kernel(dims_ref, block_ref, out_ref, low_ref, own_ref, own_high_ref):
    planes = out_ref.shape[0]
    sec_dev, size, _ = block_ref.shape
    share = size // planes
    direct_rows = low_ref.shape[1]
    for slot in range(sec_dev):
        live = live_area((size, size), 0, dims_ref[0, slot], dims_ref[1, slot])
        masked = jnp.where(live, block_ref[slot], 0.0).reshape(planes, share, size)
        here = slice(slot * share, (slot + 1) * share)
        out_ref[:, here, :] = masked
        if (slot + 1) * share <= direct_rows:
            low_ref[:, here, :] = masked
    own = out_ref[lax.axis_index("mpo")]
    own_ref[...] = own
    own_high_ref[...] = own[direct_rows:]


def mask_blocks(sector_dims, wavefunction, planes):
    sec_dev, size, _ = wavefunction.shape
    rows = sec_dev * size // planes
    shapes = ((planes, rows, size), (planes, rows // 2, size), (rows, size), (rows - rows // 2, size))
    return pl.pallas_call(
        mask_kernel,
        out_shape=[jax.ShapeDtypeStruct(shape, jnp.float32) for shape in shapes],
        in_specs=[SMEM, VMEM],
        out_specs=[VMEM] * 4,
        compiler_params=SMALL,
    )(sector_dims.T, wavefunction)


def split(value):
    high = value.astype(jnp.bfloat16)
    return high, (value - high.astype(jnp.float32)).astype(jnp.bfloat16)


def product(a, b, contract):
    dims = (((1,), (contract,)), ((), ()))
    dot = functools.partial(lax.dot_general, dimension_numbers=dims, preferred_element_type=jnp.float32)
    return dot(a[0], b[0]) + (dot(a[0], b[1]) + dot(a[1], b[0]))


def folded(value):
    while value.shape[0] > TILE:
        half = value.shape[0] // 2
        value = value[:half] + value[half:]
    return value


def halved(one, other):
    half = one.shape[1] // 2
    return jnp.concatenate([x[:, :half] + x[:, half:] for x in (one, other)], axis=1)


def terms_kernel(group, sec_dev, places, turned, last, added, meta_ref, *refs):
    operands = 1 + max(at for held, _ in places for at in held) + any(part is not None for _, part in places)
    left_ref, right_ref = refs[:2]
    sources, refs = refs[2 : 2 + operands], refs[2 + operands :]
    *refs, high_ref, low_ref, left_buf, right_buf, sems = refs
    count = meta_ref[COUNT + group]
    kinds, _, size, _ = high_ref.shape

    def env_copies(at):
        term = meta_ref[ORDER + group * TERMS_MAX + at]
        return (
            pltpu.make_async_copy(left_ref.at[term], left_buf.at[at], sems.at[0, at]),
            pltpu.make_async_copy(right_ref.at[term], right_buf.at[at], sems.at[1, at]),
        )

    @pl.loop(0, count)
    def _(at):
        for copy in env_copies(at):
            copy.start()

    others, refs = refs[:added], refs[added:]
    *pieces, total_ref = refs
    total_ref[...] = others[0][...] if added > 1 else jnp.zeros_like(total_ref)
    planes, rows, _ = total_ref.shape
    share = rows // sec_dev
    plane = lax.axis_index("mpo")

    def prepare(k, kind, held, part):
        groups = [sources[at].at[i] for at in held for i in range(sources[at].shape[0])]
        direct = sec_dev if part is None else groups[0].shape[0] // share if held else 0
        for slot in range(sec_dev):
            found = meta_ref[SOURCE + kind * sec_dev + slot]
            live = meta_ref[LIVE + kind * sec_dev + slot] != 0
            first = pl.ds(pl.multiple_of(jnp.minimum(found, max(direct, 1) - 1) * share, share), share)
            second = pl.ds(pl.multiple_of(jnp.maximum(found - direct, 0) * share, share), share)
            for r in range(planes):
                to = lax.rem(plane + (planes + AHEAD - r), planes) if turned else r
                if part is None:
                    block = groups[r][first, :]
                else:
                    block = sources[-1][to, part, second, :]
                    if direct:
                        block = jnp.where(found < direct, groups[r][first, :], block)
                high, low = split(jnp.where(live, block, 0.0))
                to = pl.ds(pl.multiple_of(to * share, share), share)
                high_ref[k, slot, to, :] = high
                low_ref[k, slot, to, :] = low

    for k, (held, part) in enumerate(places):
        kind = GROUPS[group][k]
        pl.when(meta_ref[USED + kind] != 0)(functools.partial(prepare, k, kind, held, part))

    @pl.loop(0, count)
    def _(at):
        for copy in env_copies(at):
            copy.wait()
        k = meta_ref[PICK + group * TERMS_MAX + at]
        for slot in range(sec_dev):
            middle = product(split(left_buf[at, slot]), (high_ref[k, slot], low_ref[k, slot]), 0)
            part = product(split(middle), split(right_buf[at, slot]), 1)
            total_ref[:, slot * share : (slot + 1) * share, :] += part.reshape(-1, share, size)

    if last:
        own_ref, up_ref, down_ref, far_ref, two_up_ref, two_down_ref = pieces
        if added == 1:
            sums = others[0][...]
        else:
            masked_ref = others[1]
            products = [folded(total_ref[r] * masked_ref[r]) for r in range(planes)]
            own = masked_ref[plane]
            sums = halved(sum(products), folded(own * own))
        outs = (
            (own_ref, 0), (up_ref.at[0], 1), (up_ref.at[1], 3), (down_ref.at[0], -1), (down_ref.at[1], -3),
            (far_ref, 4), (two_up_ref, 2), (two_down_ref, -2),
        )
        for out_ref, away in outs:
            out_ref[:rows, :] = total_ref[lax.rem(plane + (planes + away), planes)]
            out_ref[rows:, :] = sums


def apply_terms(group, meta, operands, places, turned, envs, others=()):
    terms, sec_dev, size, _ = envs[0].shape
    planes = sum(operands[at].shape[0] for at in places[0][0])
    rows = sec_dev * size // planes
    kinds = len(GROUPS[group])
    last = bool(others)
    total = (planes, rows, size)
    scratch = [pltpu.VMEM((kinds, sec_dev, size, size), jnp.bfloat16)] * 2
    scratch += [pltpu.VMEM(envs[0].shape, jnp.float32)] * 2
    scratch += [pltpu.SemaphoreType.DMA((2, terms))]
    if last:
        piece = (rows + TILE, size)
        outs = [piece, (2, *piece), (2, *piece), piece, piece, piece]
        scratch = [pltpu.VMEM(total, jnp.float32)] + scratch
    else:
        outs = [total]
    got = pl.pallas_call(
        functools.partial(terms_kernel, group, sec_dev, places, turned, last, len(others)),
        out_shape=[jax.ShapeDtypeStruct(shape, jnp.float32) for shape in outs],
        in_specs=[SMEM, ANY, ANY] + [VMEM] * (len(operands) + len(others)),
        out_specs=[VMEM] * len(outs),
        scratch_shapes=scratch,
        compiler_params=pltpu.CompilerParams(vmem_limit_bytes=KERNEL_VMEM),
        cost_estimate=pl.CostEstimate(
            flops=sec_dev * terms * 6 * size**3, bytes_accessed=4 * sec_dev * size * size * (terms + 4), transcendentals=0
        ),
    )(meta, *envs, *operands, *others)
    return got if last else got[0]


def middle_kernel(two_up_ref, two_down_ref, up_ref, down_ref, far_ref, sum_up_ref, sum_down_ref):
    sum_up_ref[...] = two_up_ref[...] + up_ref[1]
    sum_down_ref[...] = two_down_ref[...] + (down_ref[1] + far_ref[...])


def reduce_over_planes(pieces):
    own, up, down, far, two_up, two_down = pieces
    up = passed_along(up, "mpo", 1)
    down = passed_along(down, "mpo", -1)
    far = passed_along(far, "mpo", -2)
    shape = jax.ShapeDtypeStruct(own.shape, jnp.float32)
    sum_up, sum_down = pl.pallas_call(
        middle_kernel, out_shape=(shape, shape), in_specs=[VMEM] * 5, out_specs=(VMEM, VMEM), compiler_params=SMALL
    )(two_up, two_down, up, down, far)
    return own, up, down, passed_along(sum_up, "mpo", 2), passed_along(sum_down, "mpo", -2)


def summed(refs, here):
    own_ref, up_ref, down_ref, two_up_ref, two_down_ref = refs
    near = own_ref[here, :] + (up_ref[0, here, :] + down_ref[0, here, :])
    return near + (two_up_ref[here, :] + two_down_ref[here, :])


def sum_kernel(dims_ref, *refs):
    *parts, sigma_ref, payload_ref = refs
    rows, _ = sigma_ref.shape
    sec_dev = dims_ref.shape[1]
    share = rows // sec_dev
    first_row = lax.axis_index("mpo") * share
    for slot in range(sec_dev):
        here = slice(slot * share, (slot + 1) * share)
        total = summed(parts, here)
        live = live_area(total.shape, first_row, dims_ref[0, slot], dims_ref[1, slot])
        sigma = jnp.where(live, total, 0.0)
        sigma_ref[here, :] = sigma
        payload_ref[here, :] = sigma
    payload_ref[rows:, :] = summed(parts, slice(rows, rows + TILE))


def sum_parts(sector_dims, parts):
    rows, size = parts[0].shape
    return pl.pallas_call(
        sum_kernel,
        out_shape=(
            jax.ShapeDtypeStruct((rows - TILE, size), jnp.float32),
            jax.ShapeDtypeStruct((rows, size), jnp.float32),
        ),
        in_specs=[SMEM] + [VMEM] * 5,
        out_specs=(VMEM, VMEM),
        compiler_params=SMALL,
    )(sector_dims.T, *parts)


def pair_kernel(one_ref, other_ref, pair_ref, sums_ref):
    rows = pair_ref.shape[1]
    pair_ref[0] = one_ref[:rows, :]
    pair_ref[1] = other_ref[:rows, :]
    sums_ref[...] = one_ref[rows:, :] + other_ref[rows:, :]


def make_pair(one, other):
    rows, size = one.shape
    return pl.pallas_call(
        pair_kernel,
        out_shape=(
            jax.ShapeDtypeStruct((2, rows - TILE, size), jnp.float32),
            jax.ShapeDtypeStruct((TILE, size), jnp.float32),
        ),
        in_specs=[VMEM] * 2,
        out_specs=(VMEM, VMEM),
        compiler_params=SMALL,
    )(one, other)


def assemble_kernel(*refs):
    *pieces, full_ref = refs
    for r, piece_ref in enumerate(pieces):
        full_ref[r] = piece_ref[...]


def assemble(pieces):
    return pl.pallas_call(
        assemble_kernel,
        out_shape=jax.ShapeDtypeStruct((len(pieces), *pieces[0].shape), jnp.float32),
        in_specs=[VMEM] * len(pieces),
        out_specs=VMEM,
        compiler_params=SMALL,
    )(*pieces)


def final_kernel(dims_ref, *refs):
    parts, (sigma_ref, masked_ref, residual_ref, applied_ref) = refs[:5], refs[5:]
    sec_dev, share, size = residual_ref.shape
    first_row = lax.axis_index("mpo") * share
    sums = summed(parts, slice(sec_dev * share, sec_dev * share + TILE))
    half = size // 2
    quotient = jnp.sum(sums[:, :half], keepdims=True) / jnp.sum(sums[:, half:], keepdims=True)
    for slot in range(sec_dev):
        here = slice(slot * share, (slot + 1) * share)
        total = summed(parts, here)
        live = live_area(total.shape, first_row, dims_ref[0, slot], dims_ref[1, slot])
        sigma = sigma_ref[here, :]
        residual_ref[slot] = sigma - quotient * masked_ref[here, :]
        applied_ref[slot] = jnp.where(live, total, 0.0) - quotient * sigma


def finish(sector_dims, parts, sigma, masked):
    sec_dev = sector_dims.shape[0]
    rows, size = masked.shape
    return pl.pallas_call(
        final_kernel,
        out_shape=(jax.ShapeDtypeStruct((sec_dev, rows // sec_dev, size), jnp.float32),) * 2,
        in_specs=[SMEM] + [VMEM] * 7,
        out_specs=(VMEM, VMEM),
        compiler_params=SMALL,
    )(sector_dims.T, *parts, sigma, masked)


def spread(sums):
    devices, planes = lax.axis_size("sec"), lax.axis_size("mpo")
    step = devices // planes
    return [
        lax.ppermute(
            sums,
            ("sec", "mpo"),
            [(((i + step * m + more) % devices) * planes + m, i * planes + m) for i in range(devices) for m in range(planes)],
        )
        for more in range(step // 2)
    ]


def sent(blocks, kinds):
    return [passed_along(blocks, "sec", distance_of(kind)) for kind in kinds]


def local(wavefunction, left_env, right_env, sector_dims, charges, term_class):
    planes = lax.axis_size("mpo")
    sec_dev = wavefunction.shape[0]
    envs = (left_env, right_env)
    whole_kinds, part_kinds = GROUPS[0][1:], GROUPS[1]
    masked, low, masked_share, high_share = mask_blocks(sector_dims, wavefunction, planes)
    shares = lax.all_gather(jnp.stack(sent(high_share, part_kinds)), "mpo", axis=0)
    meta = make_plan(charges, term_class, sec_dev)
    whole, part = sent(masked, whole_kinds), sent(low, part_kinds)
    whole_places = (((0,), None), ((1,), None), ((2,), None))
    first = apply_terms(0, meta, [masked, *whole], whole_places, False, envs)
    pieces = apply_terms(1, meta, [*part, shares], (((0,), 0), ((1,), 1)), False, envs, [first, masked])
    sigma, payload = sum_parts(sector_dims, reduce_over_planes(pieces))

    pair, sums = make_pair(*sent(payload, part_kinds))
    one, back_one, two = passed_along(sigma, "mpo", 1), passed_along(sigma, "mpo", -1), passed_along(sigma, "mpo", 2)
    one, back_one, two, pair = lax.optimization_barrier((one, back_one, two, pair))
    shares = lax.all_gather(pair, "mpo", axis=0)
    near = assemble([back_one, sigma, one, two])
    near_whole = sent(near, whole_kinds)
    three, four = passed_along(two, "mpo", 1), passed_along(two, "mpo", 2)
    back_two, back_three = passed_along(back_one, "mpo", -1), passed_along(back_one, "mpo", -2)
    far = assemble([three, four, back_three, back_two])
    far_whole = sent(far, whole_kinds)
    far, sums = lax.optimization_barrier((far, sums))
    some, others = spread(sums)

    operands = [near, far, near_whole[0], far_whole[0], near_whole[1], far_whole[1], shares]
    places = (((0, 1), None), ((2, 3), None), ((4, 5), None), ((), 0), ((), 1))
    pieces = apply_terms(2, meta, operands, places, True, envs, [some + others])
    return finish(sector_dims, reduce_over_planes(pieces), sigma, masked_share)


def solution(mesh):
    placed = (
        P("sec", None, None),
        P("mpo", "sec", None, None),
        P("mpo", "sec", None, None),
        P("sec", None),
        P(),
        P("mpo"),
    )
    return jax.shard_map(
        local,
        mesh=mesh,
        in_specs=placed,
        out_specs=(P("sec", "mpo", None), P("sec", "mpo", None)),
        check_vma=False,
    )
```

```python
import functools
import jax
import jax.numpy as jnp
from jax import lax
from jax.experimental import pallas as pl
from jax.experimental.pallas import tpu as pltpu
from jax.sharding import PartitionSpec as P

number_steps = (0, 1, 1, -1, -1)
spin_steps = (0, 1, -1, 1, -1)
SPINS = 8
GROUPS = ((0, 2, 3), (1, 4))
SOURCE, LIVE, COUNT, ORDER, PICK, USED, META = 0, 32, 64, 72, 104, 136, 144
TERMS_MAX = 8
TILE = 8
AHEAD = 1
SMEM = pl.BlockSpec(memory_space=pltpu.SMEM)
VMEM = pl.BlockSpec(memory_space=pltpu.VMEM)
ANY = pl.BlockSpec(memory_space=pl.ANY)
KERNEL_VMEM = 47 * 2**20
SMALL = pltpu.CompilerParams(vmem_limit_bytes=8 * 2**20)


def distance_of(kind):
    return SPINS * number_steps[kind] + spin_steps[kind]


def passed_along(value, axis, by):
    count = lax.axis_size(axis)
    return lax.ppermute(value, axis, [(i, (i + by) % count) for i in range(count)])


def plan_kernel(sec_dev, charges_ref, term_ref, meta_ref):
    devices = charges_ref.shape[1] // sec_dev
    here = lax.axis_index("sec")
    for kind in range(5):
        sender = lax.rem(here + (devices - distance_of(kind) % devices), devices)
        for slot in range(sec_dev):
            number = charges_ref[0, here * sec_dev + slot] - number_steps[kind]
            spin = charges_ref[1, here * sec_dev + slot] - spin_steps[kind]
            found, live = jnp.int32(0), jnp.int32(0)
            for other in range(sec_dev):
                same = (charges_ref[0, sender * sec_dev + other] == number) & (
                    charges_ref[1, sender * sec_dev + other] == spin
                )
                found = jnp.where(same, other, found)
                live = jnp.where(same, 1, live)
            meta_ref[SOURCE + kind * sec_dev + slot] = found
            meta_ref[LIVE + kind * sec_dev + slot] = live
    counts = [jnp.int32(0) for _ in GROUPS]
    for kind in range(5):
        used = jnp.int32(0)
        for term in range(term_ref.shape[0]):
            used = jnp.where(term_ref[term] == kind, 1, used)
        meta_ref[USED + kind] = used
    for term in range(term_ref.shape[0]):
        kind = term_ref[term]
        for g, group in enumerate(GROUPS):
            inside, pick = kind == group[0], jnp.int32(0)
            for place, member in enumerate(group[1:], 1):
                inside = inside | (kind == member)
                pick = jnp.where(kind == member, place, pick)
            at = counts[g]
            keep_order = meta_ref[ORDER + g * TERMS_MAX + at]
            keep_pick = meta_ref[PICK + g * TERMS_MAX + at]
            meta_ref[ORDER + g * TERMS_MAX + at] = jnp.where(inside, term, keep_order)
            meta_ref[PICK + g * TERMS_MAX + at] = jnp.where(inside, pick, keep_pick)
            counts[g] = jnp.where(inside, at + 1, at)
    for g in range(len(GROUPS)):
        meta_ref[COUNT + g] = counts[g]


def make_plan(charges, term_class, sec_dev):
    return pl.pallas_call(
        functools.partial(plan_kernel, sec_dev),
        out_shape=jax.ShapeDtypeStruct((META,), jnp.int32),
        in_specs=[SMEM] * 2,
        out_specs=SMEM,
        compiler_params=SMALL,
    )(charges.T, term_class)


def live_area(shape, first_row, rows, cols):
    row = lax.broadcasted_iota(jnp.int32, shape, len(shape) - 2) + first_row
    col = lax.broadcasted_iota(jnp.int32, shape, len(shape) - 1)
    return (row < rows) & (col < cols)


def mask_kernel(dims_ref, block_ref, out_ref, low_ref, own_ref, own_high_ref):
    planes = out_ref.shape[0]
    sec_dev, size, _ = block_ref.shape
    share = size // planes
    direct_rows = low_ref.shape[1]
    for slot in range(sec_dev):
        live = live_area((size, size), 0, dims_ref[0, slot], dims_ref[1, slot])
        masked = jnp.where(live, block_ref[slot], 0.0).reshape(planes, share, size)
        here = slice(slot * share, (slot + 1) * share)
        out_ref[:, here, :] = masked
        if (slot + 1) * share <= direct_rows:
            low_ref[:, here, :] = masked
    own = out_ref[lax.axis_index("mpo")]
    own_ref[...] = own
    own_high_ref[...] = own[direct_rows:]


def mask_blocks(sector_dims, wavefunction, planes):
    sec_dev, size, _ = wavefunction.shape
    rows = sec_dev * size // planes
    shapes = ((planes, rows, size), (planes, rows // 2, size), (rows, size), (rows - rows // 2, size))
    return pl.pallas_call(
        mask_kernel,
        out_shape=[jax.ShapeDtypeStruct(shape, jnp.float32) for shape in shapes],
        in_specs=[SMEM, VMEM],
        out_specs=[VMEM] * 4,
        compiler_params=SMALL,
    )(sector_dims.T, wavefunction)


def split(value):
    high = value.astype(jnp.bfloat16)
    return high, (value - high.astype(jnp.float32)).astype(jnp.bfloat16)


def product(a, b, contract):
    dims = (((1,), (contract,)), ((), ()))
    dot = functools.partial(lax.dot_general, dimension_numbers=dims, preferred_element_type=jnp.float32)
    return dot(a[0], b[0]) + (dot(a[0], b[1]) + dot(a[1], b[0]))


def folded(value):
    while value.shape[0] > TILE:
        half = value.shape[0] // 2
        value = value[:half] + value[half:]
    return value


def halved(one, other):
    half = one.shape[1] // 2
    return jnp.concatenate([x[:, :half] + x[:, half:] for x in (one, other)], axis=1)


def terms_kernel(group, sec_dev, places, turned, last, added, operands, shared, meta_ref, *refs):
    left_ref, right_ref = refs[:2]
    sources, refs = refs[2 : 2 + operands], refs[2 + operands :]
    sources, shares = sources[: operands - shared], sources[operands - shared :]
    *refs, high_ref, low_ref, left_buf, right_buf, sems = refs
    count = meta_ref[COUNT + group]
    kinds, _, size, _ = high_ref.shape

    def env_copies(at):
        term = meta_ref[ORDER + group * TERMS_MAX + at]
        return (
            pltpu.make_async_copy(left_ref.at[term], left_buf.at[at], sems.at[0, at]),
            pltpu.make_async_copy(right_ref.at[term], right_buf.at[at], sems.at[1, at]),
        )

    @pl.loop(0, count)
    def _(at):
        for copy in env_copies(at):
            copy.start()

    others, refs = refs[:added], refs[added:]
    *pieces, total_ref = refs
    total_ref[...] = others[0][...] if added > 1 else jnp.zeros_like(total_ref)
    planes, rows, _ = total_ref.shape
    share = rows // sec_dev
    plane = lax.axis_index("mpo")

    def prepare(k, kind, held, part):
        groups = [sources[at].at[i] for at in held for i in range(sources[at].shape[0])]
        direct = sec_dev if part is None else groups[0].shape[0] // share
        for slot in range(sec_dev):
            found = meta_ref[SOURCE + kind * sec_dev + slot]
            live = meta_ref[LIVE + kind * sec_dev + slot] != 0
            first = pl.ds(pl.multiple_of(jnp.minimum(found, direct - 1) * share, share), share)
            second = pl.ds(pl.multiple_of(jnp.maximum(found - direct, 0) * share, share), share)
            for r in range(planes):
                to = r if part is None and not turned else lax.rem(plane + (planes + AHEAD - r), planes)
                if part is None or turned:
                    block = groups[r][first, :]
                else:
                    block = sources[held[0]][to, first, :]
                if part is not None:
                    block = jnp.where(found < direct, block, shares[r][part, second, :])
                high, low = split(jnp.where(live, block, 0.0))
                to = pl.ds(pl.multiple_of(to * share, share), share)
                high_ref[k, slot, to, :] = high
                low_ref[k, slot, to, :] = low

    for k, (held, part) in enumerate(places):
        kind = GROUPS[group][k]
        pl.when(meta_ref[USED + kind] != 0)(functools.partial(prepare, k, kind, held, part))

    @pl.loop(0, count)
    def _(at):
        for copy in env_copies(at):
            copy.wait()
        k = meta_ref[PICK + group * TERMS_MAX + at]
        for slot in range(sec_dev):
            middle = product(split(left_buf[at, slot]), (high_ref[k, slot], low_ref[k, slot]), 0)
            part = product(split(middle), split(right_buf[at, slot]), 1)
            total_ref[:, slot * share : (slot + 1) * share, :] += part.reshape(-1, share, size)

    if last:
        own_ref, up_ref, down_ref, far_ref, two_up_ref, two_down_ref = pieces
        if len(others[1].shape) == 2:
            sums = others[1][...]
        else:
            masked_ref = others[1]
            products = [folded(total_ref[r] * masked_ref[r]) for r in range(planes)]
            own = masked_ref[plane]
            sums = halved(sum(products), folded(own * own))
        outs = (
            (own_ref, 0), (up_ref.at[0], 1), (up_ref.at[1], 3), (down_ref.at[0], -1), (down_ref.at[1], -3),
            (far_ref, 4), (two_up_ref, 2), (two_down_ref, -2),
        )
        for out_ref, away in outs:
            out_ref[:rows, :] = total_ref[lax.rem(plane + (planes + away), planes)]
            out_ref[rows:, :] = sums


def apply_terms(group, meta, operands, shares, places, turned, envs, others=()):
    terms, sec_dev, size, _ = envs[0].shape
    planes = sum(operands[at].shape[0] for at in places[0][0])
    rows = sec_dev * size // planes
    kinds = len(GROUPS[group])
    last = bool(others)
    total = (planes, rows, size)
    scratch = [pltpu.VMEM((kinds, sec_dev, size, size), jnp.bfloat16)] * 2
    scratch += [pltpu.VMEM(envs[0].shape, jnp.float32)] * 2
    scratch += [pltpu.SemaphoreType.DMA((2, terms))]
    if last:
        piece = (rows + TILE, size)
        outs = [piece, (2, *piece), (2, *piece), piece, piece, piece]
        scratch = [pltpu.VMEM(total, jnp.float32)] + scratch
    else:
        outs = [total]
    got = pl.pallas_call(
        functools.partial(
            terms_kernel, group, sec_dev, places, turned, last, len(others), len(operands) + len(shares), len(shares)
        ),
        out_shape=[jax.ShapeDtypeStruct(shape, jnp.float32) for shape in outs],
        in_specs=[SMEM, ANY, ANY] + [VMEM] * (len(operands) + len(shares) + len(others)),
        out_specs=[VMEM] * len(outs),
        scratch_shapes=scratch,
        compiler_params=pltpu.CompilerParams(vmem_limit_bytes=KERNEL_VMEM),
        cost_estimate=pl.CostEstimate(
            flops=sec_dev * terms * 6 * size**3, bytes_accessed=4 * sec_dev * size * size * (terms + 4), transcendentals=0
        ),
    )(meta, *envs, *operands, *shares, *others)
    return got if last else got[0]


def middle_kernel(two_up_ref, two_down_ref, up_ref, down_ref, far_ref, sum_up_ref, sum_down_ref):
    sum_up_ref[...] = two_up_ref[...] + up_ref[1]
    sum_down_ref[...] = two_down_ref[...] + (down_ref[1] + far_ref[...])


def reduce_over_planes(pieces):
    own, up, down, far, two_up, two_down = pieces
    up = passed_along(up, "mpo", 1)
    down = passed_along(down, "mpo", -1)
    far = passed_along(far, "mpo", -2)
    shape = jax.ShapeDtypeStruct(own.shape, jnp.float32)
    sum_up, sum_down = pl.pallas_call(
        middle_kernel, out_shape=(shape, shape), in_specs=[VMEM] * 5, out_specs=(VMEM, VMEM), compiler_params=SMALL
    )(two_up, two_down, up, down, far)
    return own, up, down, passed_along(sum_up, "mpo", 2), passed_along(sum_down, "mpo", -2)


def summed(refs, here):
    own_ref, up_ref, down_ref, two_up_ref, two_down_ref = refs
    near = own_ref[here, :] + (up_ref[0, here, :] + down_ref[0, here, :])
    return near + (two_up_ref[here, :] + two_down_ref[here, :])


def sum_kernel(dims_ref, *refs):
    *parts, sigma_ref, payload_ref = refs
    rows, _ = sigma_ref.shape
    sec_dev = dims_ref.shape[1]
    share = rows // sec_dev
    first_row = lax.axis_index("mpo") * share
    for slot in range(sec_dev):
        here = slice(slot * share, (slot + 1) * share)
        total = summed(parts, here)
        live = live_area(total.shape, first_row, dims_ref[0, slot], dims_ref[1, slot])
        sigma = jnp.where(live, total, 0.0)
        sigma_ref[here, :] = sigma
    high_rows = payload_ref.shape[0] - TILE
    payload_ref[:high_rows, :] = sigma_ref[rows - high_rows :, :]
    payload_ref[high_rows:, :] = summed(parts, slice(rows, rows + TILE))


def sum_parts(sector_dims, parts):
    rows, size = parts[0].shape
    rows -= TILE
    return pl.pallas_call(
        sum_kernel,
        out_shape=(
            jax.ShapeDtypeStruct((rows, size), jnp.float32),
            jax.ShapeDtypeStruct((rows - rows // 2 + TILE, size), jnp.float32),
        ),
        in_specs=[SMEM] + [VMEM] * 5,
        out_specs=(VMEM, VMEM),
        compiler_params=SMALL,
    )(sector_dims.T, *parts)


def pair_kernel(one_ref, other_ref, pair_ref, sums_ref):
    rows = pair_ref.shape[1]
    pair_ref[0] = one_ref[:rows, :]
    pair_ref[1] = other_ref[:rows, :]
    sums_ref[...] = one_ref[rows:, :] + other_ref[rows:, :]


def make_pair(one, other):
    rows, size = one.shape
    return pl.pallas_call(
        pair_kernel,
        out_shape=(
            jax.ShapeDtypeStruct((2, rows - TILE, size), jnp.float32),
            jax.ShapeDtypeStruct((TILE, size), jnp.float32),
        ),
        in_specs=[VMEM] * 2,
        out_specs=(VMEM, VMEM),
        compiler_params=SMALL,
    )(one, other)


def assemble_kernel(*refs):
    *pieces, full_ref, low_ref = refs
    rows = low_ref.shape[1]
    for r, piece_ref in enumerate(pieces):
        full_ref[r] = piece_ref[...]
        low_ref[r] = piece_ref[:rows, :]


def assemble(pieces):
    rows, size = pieces[0].shape
    shapes = ((len(pieces), rows, size), (len(pieces), rows // 2, size))
    return pl.pallas_call(
        assemble_kernel,
        out_shape=[jax.ShapeDtypeStruct(shape, jnp.float32) for shape in shapes],
        in_specs=[VMEM] * len(pieces),
        out_specs=[VMEM] * 2,
        compiler_params=SMALL,
    )(*pieces)


def final_kernel(dims_ref, *refs):
    parts, (sigma_ref, masked_ref, residual_ref, applied_ref) = refs[:5], refs[5:]
    sec_dev, share, size = residual_ref.shape
    first_row = lax.axis_index("mpo") * share
    sums = summed(parts, slice(sec_dev * share, sec_dev * share + TILE))
    half = size // 2
    quotient = jnp.sum(sums[:, :half], keepdims=True) / jnp.sum(sums[:, half:], keepdims=True)
    for slot in range(sec_dev):
        here = slice(slot * share, (slot + 1) * share)
        total = summed(parts, here)
        live = live_area(total.shape, first_row, dims_ref[0, slot], dims_ref[1, slot])
        sigma = sigma_ref[here, :]
        residual_ref[slot] = sigma - quotient * masked_ref[here, :]
        applied_ref[slot] = jnp.where(live, total, 0.0) - quotient * sigma


def finish(sector_dims, parts, sigma, masked):
    sec_dev = sector_dims.shape[0]
    rows, size = masked.shape
    return pl.pallas_call(
        final_kernel,
        out_shape=(jax.ShapeDtypeStruct((sec_dev, rows // sec_dev, size), jnp.float32),) * 2,
        in_specs=[SMEM] + [VMEM] * 7,
        out_specs=(VMEM, VMEM),
        compiler_params=SMALL,
    )(sector_dims.T, *parts, sigma, masked)


def spread(sums):
    devices, planes = lax.axis_size("sec"), lax.axis_size("mpo")
    step = devices // planes
    return [
        lax.ppermute(
            sums,
            ("sec", "mpo"),
            [(((i + step * m + more) % devices) * planes + m, i * planes + m) for i in range(devices) for m in range(planes)],
        )
        for more in range(step // 2)
    ]


def sent(blocks, kinds):
    return [passed_along(blocks, "sec", distance_of(kind)) for kind in kinds]


def first_round(share):
    return passed_along(share, "mpo", 1), passed_along(share, "mpo", -1), passed_along(share, "mpo", 2)


def second_round(one, back_one, two):
    three, four = passed_along(two, "mpo", 1), passed_along(two, "mpo", 2)
    return three, four, passed_along(back_one, "mpo", -2), passed_along(back_one, "mpo", -1)


def both_calls(meta, blocks, low, pair, turned, envs, others):
    blocks, pair = lax.optimization_barrier((blocks, pair))
    whole = sent(blocks, GROUPS[0][1:])
    one, back_one, two = first_round(pair)
    one, back_one, two, low = lax.optimization_barrier((one, back_one, two, low))
    part = sent(low, GROUPS[1])
    shares = [back_one, pair, one, two, *second_round(one, back_one, two)]
    total = apply_terms(0, meta, [blocks, *whole], [], (((0,), None), ((1,), None), ((2,), None)), turned, envs)
    return apply_terms(1, meta, part, shares, (((0,), 0), ((1,), 1)), turned, envs, [total, *others])


def local(wavefunction, left_env, right_env, sector_dims, charges, term_class):
    planes = lax.axis_size("mpo")
    sec_dev = wavefunction.shape[0]
    envs = (left_env, right_env)
    masked, low, masked_share, high_share = mask_blocks(sector_dims, wavefunction, planes)
    pair = jnp.stack(sent(high_share, GROUPS[1]))
    meta = make_plan(charges, term_class, sec_dev)
    pieces = both_calls(meta, masked, low, pair, False, envs, [masked])
    sigma, payload = sum_parts(sector_dims, reduce_over_planes(pieces))

    pair, sums = make_pair(*sent(payload, GROUPS[1]))
    one, back_one, two = first_round(sigma)
    some, more = spread(sums)
    full, low = assemble([back_one, sigma, one, two, *second_round(one, back_one, two)])
    full, pair, some, more = lax.optimization_barrier((full, pair, some, more))

    pieces = both_calls(meta, full, low, pair, True, envs, [some + more])
    return finish(sector_dims, reduce_over_planes(pieces), sigma, masked_share)


def solution(mesh):
    placed = (
        P("sec", None, None),
        P("mpo", "sec", None, None),
        P("mpo", "sec", None, None),
        P("sec", None),
        P(),
        P("mpo"),
    )
    return jax.shard_map(
        local,
        mesh=mesh,
        in_specs=placed,
        out_specs=(P("sec", "mpo", None), P("sec", "mpo", None)),
        check_vma=False,
    )
```

```python
import functools
import jax
import jax.numpy as jnp
from jax import lax
from jax.experimental import pallas as pl
from jax.experimental.pallas import tpu as pltpu
from jax.sharding import PartitionSpec as P

number_steps = (0, 1, 1, -1, -1)
spin_steps = (0, 1, -1, 1, -1)
SPINS = 8
GROUPS = ((0, 2, 3), (1, 4))
SOURCE, LIVE, COUNT, ORDER, PICK, USED, META = 0, 32, 64, 72, 104, 136, 144
TERMS_MAX = 8
TILE = 8
AHEAD = 1
SMEM = pl.BlockSpec(memory_space=pltpu.SMEM)
VMEM = pl.BlockSpec(memory_space=pltpu.VMEM)
ANY = pl.BlockSpec(memory_space=pl.ANY)
KERNEL_VMEM = 47 * 2**20
SMALL = pltpu.CompilerParams(vmem_limit_bytes=8 * 2**20)


def distance_of(kind):
    return SPINS * number_steps[kind] + spin_steps[kind]


def passed_along(value, axis, by):
    count = lax.axis_size(axis)
    return lax.ppermute(value, axis, [(i, (i + by) % count) for i in range(count)])


def plan_kernel(sec_dev, charges_ref, term_ref, meta_ref):
    devices = charges_ref.shape[1] // sec_dev
    here = lax.axis_index("sec")
    for kind in range(5):
        sender = lax.rem(here + (devices - distance_of(kind) % devices), devices)
        for slot in range(sec_dev):
            number = charges_ref[0, here * sec_dev + slot] - number_steps[kind]
            spin = charges_ref[1, here * sec_dev + slot] - spin_steps[kind]
            found, live = jnp.int32(0), jnp.int32(0)
            for other in range(sec_dev):
                same = (charges_ref[0, sender * sec_dev + other] == number) & (
                    charges_ref[1, sender * sec_dev + other] == spin
                )
                found = jnp.where(same, other, found)
                live = jnp.where(same, 1, live)
            meta_ref[SOURCE + kind * sec_dev + slot] = found
            meta_ref[LIVE + kind * sec_dev + slot] = live
    counts = [jnp.int32(0) for _ in GROUPS]
    for kind in range(5):
        used = jnp.int32(0)
        for term in range(term_ref.shape[0]):
            used = jnp.where(term_ref[term] == kind, 1, used)
        meta_ref[USED + kind] = used
    for term in range(term_ref.shape[0]):
        kind = term_ref[term]
        for g, group in enumerate(GROUPS):
            inside, pick = kind == group[0], jnp.int32(0)
            for place, member in enumerate(group[1:], 1):
                inside = inside | (kind == member)
                pick = jnp.where(kind == member, place, pick)
            at = counts[g]
            keep_order = meta_ref[ORDER + g * TERMS_MAX + at]
            keep_pick = meta_ref[PICK + g * TERMS_MAX + at]
            meta_ref[ORDER + g * TERMS_MAX + at] = jnp.where(inside, term, keep_order)
            meta_ref[PICK + g * TERMS_MAX + at] = jnp.where(inside, pick, keep_pick)
            counts[g] = jnp.where(inside, at + 1, at)
    for g in range(len(GROUPS)):
        meta_ref[COUNT + g] = counts[g]


def make_plan(charges, term_class, sec_dev):
    return pl.pallas_call(
        functools.partial(plan_kernel, sec_dev),
        out_shape=jax.ShapeDtypeStruct((META,), jnp.int32),
        in_specs=[SMEM] * 2,
        out_specs=SMEM,
        compiler_params=SMALL,
    )(charges.T, term_class)


def live_area(shape, first_row, rows, cols):
    row = lax.broadcasted_iota(jnp.int32, shape, len(shape) - 2) + first_row
    col = lax.broadcasted_iota(jnp.int32, shape, len(shape) - 1)
    return (row < rows) & (col < cols)


def mask_kernel(dims_ref, block_ref, out_ref, low_ref, own_ref, own_high_ref):
    planes = out_ref.shape[0]
    sec_dev, size, _ = block_ref.shape
    share = size // planes
    direct_rows = low_ref.shape[1]
    for slot in range(sec_dev):
        live = live_area((size, size), 0, dims_ref[0, slot], dims_ref[1, slot])
        masked = jnp.where(live, block_ref[slot], 0.0).reshape(planes, share, size)
        here = slice(slot * share, (slot + 1) * share)
        out_ref[:, here, :] = masked
        if (slot + 1) * share <= direct_rows:
            low_ref[:, here, :] = masked
    own = out_ref[lax.axis_index("mpo")]
    own_ref[...] = own
    own_high_ref[...] = own[direct_rows:]


def mask_blocks(sector_dims, wavefunction, planes):
    sec_dev, size, _ = wavefunction.shape
    rows = sec_dev * size // planes
    shapes = ((planes, rows, size), (planes, rows // 2, size), (rows, size), (rows - rows // 2, size))
    return pl.pallas_call(
        mask_kernel,
        out_shape=[jax.ShapeDtypeStruct(shape, jnp.float32) for shape in shapes],
        in_specs=[SMEM, VMEM],
        out_specs=[VMEM] * 4,
        compiler_params=SMALL,
    )(sector_dims.T, wavefunction)


def split(value):
    high = value.astype(jnp.bfloat16)
    return high, (value - high.astype(jnp.float32)).astype(jnp.bfloat16)


def product(a, b, contract):
    dims = (((1,), (contract,)), ((), ()))
    dot = functools.partial(lax.dot_general, dimension_numbers=dims, preferred_element_type=jnp.float32)
    return dot(a[0], b[0]) + (dot(a[0], b[1]) + dot(a[1], b[0]))


def folded(value):
    while value.shape[0] > TILE:
        half = value.shape[0] // 2
        value = value[:half] + value[half:]
    return value


def halved(one, other):
    half = one.shape[1] // 2
    return jnp.concatenate([x[:, :half] + x[:, half:] for x in (one, other)], axis=1)


def terms_kernel(group, sec_dev, places, turned, last, added, operands, shared, meta_ref, *refs):
    left_ref, right_ref = refs[:2]
    sources, refs = refs[2 : 2 + operands], refs[2 + operands :]
    sources, shares = sources[: operands - shared], sources[operands - shared :]
    *refs, high_ref, low_ref, left_buf, right_buf, sems = refs
    count = meta_ref[COUNT + group]
    kinds, _, size, _ = high_ref.shape

    def env_copies(at):
        term = meta_ref[ORDER + group * TERMS_MAX + at]
        return (
            pltpu.make_async_copy(left_ref.at[term], left_buf.at[at], sems.at[0, at]),
            pltpu.make_async_copy(right_ref.at[term], right_buf.at[at], sems.at[1, at]),
        )

    @pl.loop(0, count)
    def _(at):
        for copy in env_copies(at):
            copy.start()

    others, refs = refs[:added], refs[added:]
    *pieces, total_ref = refs
    total_ref[...] = others[0][...] if added > 1 else jnp.zeros_like(total_ref)
    planes, rows, _ = total_ref.shape
    share = rows // sec_dev
    plane = lax.axis_index("mpo")

    def prepare(k, kind, held, part):
        groups = [sources[at].at[i] for at in held for i in range(sources[at].shape[0])]
        direct = sec_dev if part is None else groups[0].shape[0] // share
        for slot in range(sec_dev):
            found = meta_ref[SOURCE + kind * sec_dev + slot]
            live = meta_ref[LIVE + kind * sec_dev + slot] != 0
            first = pl.ds(pl.multiple_of(jnp.minimum(found, direct - 1) * share, share), share)
            second = pl.ds(pl.multiple_of(jnp.maximum(found - direct, 0) * share, share), share)
            for r in range(planes):
                to = r if part is None and not turned else lax.rem(plane + (planes + AHEAD - r), planes)
                if part is None or turned:
                    block = groups[r][first, :]
                else:
                    block = sources[held[0]][to, first, :]
                if part is not None:
                    block = jnp.where(found < direct, block, shares[r][part, second, :])
                high, low = split(jnp.where(live, block, 0.0))
                to = pl.ds(pl.multiple_of(to * share, share), share)
                high_ref[k, slot, to, :] = high
                low_ref[k, slot, to, :] = low

    for k, (held, part) in enumerate(places):
        kind = GROUPS[group][k]
        pl.when(meta_ref[USED + kind] != 0)(functools.partial(prepare, k, kind, held, part))

    @pl.loop(0, count)
    def _(at):
        for copy in env_copies(at):
            copy.wait()
        k = meta_ref[PICK + group * TERMS_MAX + at]
        for slot in range(sec_dev):
            middle = product(split(left_buf[at, slot]), (high_ref[k, slot], low_ref[k, slot]), 0)
            part = product(split(middle), split(right_buf[at, slot]), 1)
            total_ref[:, slot * share : (slot + 1) * share, :] += part.reshape(-1, share, size)

    if last:
        own_ref, up_ref, down_ref, far_up_ref, far_down_ref, two_up_ref, two_down_ref = pieces
        if len(others[1].shape) == 2:
            sums = others[1][...]
        else:
            masked_ref = others[1]
            products = [folded(total_ref[r] * masked_ref[r]) for r in range(planes)]
            own = masked_ref[plane]
            sums = halved(sum(products), folded(own * own))
        outs = (
            (own_ref, 0), (up_ref.at[0], 1), (up_ref.at[1], 3), (down_ref.at[0], -1), (down_ref.at[1], -3),
            (two_up_ref, 2), (two_down_ref, -2),
        )
        for out_ref, away in outs:
            out_ref[:rows, :] = total_ref[lax.rem(plane + (planes + away), planes)]
            out_ref[rows:, :] = sums
        half = far_up_ref.shape[0]
        opposite = total_ref[lax.rem(plane + planes // 2, planes)]
        far_up_ref[...] = opposite[:half]
        far_down_ref[: rows - half, :] = opposite[half:]
        far_down_ref[rows - half :, :] = sums


def apply_terms(group, meta, operands, shares, places, turned, envs, others=()):
    terms, sec_dev, size, _ = envs[0].shape
    planes = sum(operands[at].shape[0] for at in places[0][0])
    rows = sec_dev * size // planes
    kinds = len(GROUPS[group])
    last = bool(others)
    total = (planes, rows, size)
    scratch = [pltpu.VMEM((kinds, sec_dev, size, size), jnp.bfloat16)] * 2
    scratch += [pltpu.VMEM(envs[0].shape, jnp.float32)] * 2
    scratch += [pltpu.SemaphoreType.DMA((2, terms))]
    if last:
        piece = (rows + TILE, size)
        half = rows // 2
        outs = [piece, (2, *piece), (2, *piece), (half, size), (piece[0] - half, size), piece, piece]
        scratch = [pltpu.VMEM(total, jnp.float32)] + scratch
    else:
        outs = [total]
    got = pl.pallas_call(
        functools.partial(
            terms_kernel, group, sec_dev, places, turned, last, len(others), len(operands) + len(shares), len(shares)
        ),
        out_shape=[jax.ShapeDtypeStruct(shape, jnp.float32) for shape in outs],
        in_specs=[SMEM, ANY, ANY] + [VMEM] * (len(operands) + len(shares) + len(others)),
        out_specs=[VMEM] * len(outs),
        scratch_shapes=scratch,
        compiler_params=pltpu.CompilerParams(vmem_limit_bytes=KERNEL_VMEM),
        cost_estimate=pl.CostEstimate(
            flops=sec_dev * terms * 6 * size**3, bytes_accessed=4 * sec_dev * size * size * (terms + 4), transcendentals=0
        ),
    )(meta, *envs, *operands, *shares, *others)
    return got if last else got[0]


def middle_kernel(two_up_ref, two_down_ref, up_ref, down_ref, far_up_ref, far_down_ref, sum_up_ref, sum_down_ref):
    half = far_up_ref.shape[0]
    sum_up_ref[:half, :] = two_up_ref[:half, :] + (up_ref[1, :half, :] + far_up_ref[...])
    sum_up_ref[half:, :] = two_up_ref[half:, :] + up_ref[1, half:, :]
    sum_down_ref[:half, :] = two_down_ref[:half, :] + down_ref[1, :half, :]
    sum_down_ref[half:, :] = two_down_ref[half:, :] + (down_ref[1, half:, :] + far_down_ref[...])


def reduce_over_planes(pieces):
    own, up, down, far_up, far_down, two_up, two_down = pieces
    far_up = passed_along(far_up, "mpo", 2)
    far_down = passed_along(far_down, "mpo", -2)
    up = passed_along(up, "mpo", 1)
    down = passed_along(down, "mpo", -1)
    shape = jax.ShapeDtypeStruct(own.shape, jnp.float32)
    sum_up, sum_down = pl.pallas_call(
        middle_kernel,
        out_shape=(shape, shape),
        in_specs=[VMEM] * 6,
        out_specs=(VMEM, VMEM),
        compiler_params=SMALL,
    )(two_up, two_down, up, down, far_up, far_down)
    return own, up, down, passed_along(sum_up, "mpo", 2), passed_along(sum_down, "mpo", -2)


def summed(refs, here):
    own_ref, up_ref, down_ref, two_up_ref, two_down_ref = refs
    near = own_ref[here, :] + (up_ref[0, here, :] + down_ref[0, here, :])
    return near + (two_up_ref[here, :] + two_down_ref[here, :])


def sum_kernel(dims_ref, *refs):
    *parts, sigma_ref, payload_ref = refs
    rows, _ = sigma_ref.shape
    sec_dev = dims_ref.shape[1]
    share = rows // sec_dev
    first_row = lax.axis_index("mpo") * share
    for slot in range(sec_dev):
        here = slice(slot * share, (slot + 1) * share)
        total = summed(parts, here)
        live = live_area(total.shape, first_row, dims_ref[0, slot], dims_ref[1, slot])
        sigma = jnp.where(live, total, 0.0)
        sigma_ref[here, :] = sigma
    high_rows = payload_ref.shape[0] - TILE
    payload_ref[:high_rows, :] = sigma_ref[rows - high_rows :, :]
    payload_ref[high_rows:, :] = summed(parts, slice(rows, rows + TILE))


def sum_parts(sector_dims, parts):
    rows, size = parts[0].shape
    rows -= TILE
    return pl.pallas_call(
        sum_kernel,
        out_shape=(
            jax.ShapeDtypeStruct((rows, size), jnp.float32),
            jax.ShapeDtypeStruct((rows - rows // 2 + TILE, size), jnp.float32),
        ),
        in_specs=[SMEM] + [VMEM] * 5,
        out_specs=(VMEM, VMEM),
        compiler_params=SMALL,
    )(sector_dims.T, *parts)


def pair_kernel(one_ref, other_ref, pair_ref, sums_ref):
    rows = pair_ref.shape[1]
    pair_ref[0] = one_ref[:rows, :]
    pair_ref[1] = other_ref[:rows, :]
    sums_ref[...] = one_ref[rows:, :] + other_ref[rows:, :]


def make_pair(one, other):
    rows, size = one.shape
    return pl.pallas_call(
        pair_kernel,
        out_shape=(
            jax.ShapeDtypeStruct((2, rows - TILE, size), jnp.float32),
            jax.ShapeDtypeStruct((TILE, size), jnp.float32),
        ),
        in_specs=[VMEM] * 2,
        out_specs=(VMEM, VMEM),
        compiler_params=SMALL,
    )(one, other)


def assemble_kernel(*refs):
    *pieces, full_ref, low_ref = refs
    rows = low_ref.shape[1]
    for r, piece_ref in enumerate(pieces):
        full_ref[r] = piece_ref[...]
        low_ref[r] = piece_ref[:rows, :]


def assemble(pieces):
    rows, size = pieces[0].shape
    shapes = ((len(pieces), rows, size), (len(pieces), rows // 2, size))
    return pl.pallas_call(
        assemble_kernel,
        out_shape=[jax.ShapeDtypeStruct(shape, jnp.float32) for shape in shapes],
        in_specs=[VMEM] * len(pieces),
        out_specs=[VMEM] * 2,
        compiler_params=SMALL,
    )(*pieces)


def final_kernel(dims_ref, *refs):
    parts, (sigma_ref, masked_ref, residual_ref, applied_ref) = refs[:5], refs[5:]
    sec_dev, share, size = residual_ref.shape
    first_row = lax.axis_index("mpo") * share
    sums = summed(parts, slice(sec_dev * share, sec_dev * share + TILE))
    half = size // 2
    quotient = jnp.sum(sums[:, :half], keepdims=True) / jnp.sum(sums[:, half:], keepdims=True)
    for slot in range(sec_dev):
        here = slice(slot * share, (slot + 1) * share)
        total = summed(parts, here)
        live = live_area(total.shape, first_row, dims_ref[0, slot], dims_ref[1, slot])
        sigma = sigma_ref[here, :]
        residual_ref[slot] = sigma - quotient * masked_ref[here, :]
        applied_ref[slot] = jnp.where(live, total, 0.0) - quotient * sigma


def finish(sector_dims, parts, sigma, masked):
    sec_dev = sector_dims.shape[0]
    rows, size = masked.shape
    return pl.pallas_call(
        final_kernel,
        out_shape=(jax.ShapeDtypeStruct((sec_dev, rows // sec_dev, size), jnp.float32),) * 2,
        in_specs=[SMEM] + [VMEM] * 7,
        out_specs=(VMEM, VMEM),
        compiler_params=SMALL,
    )(sector_dims.T, *parts, sigma, masked)


def spread(sums):
    devices, planes = lax.axis_size("sec"), lax.axis_size("mpo")
    step = devices // planes
    return [
        lax.ppermute(
            sums,
            ("sec", "mpo"),
            [(((i + step * m + more) % devices) * planes + m, i * planes + m) for i in range(devices) for m in range(planes)],
        )
        for more in range(step // 2)
    ]


def sent(blocks, kinds):
    return [passed_along(blocks, "sec", distance_of(kind)) for kind in kinds]


def first_round(share):
    return passed_along(share, "mpo", 1), passed_along(share, "mpo", -1), passed_along(share, "mpo", 2)


def second_round(one, back_one, two):
    three, four = passed_along(two, "mpo", 1), passed_along(two, "mpo", 2)
    return three, four, passed_along(back_one, "mpo", -2), passed_along(back_one, "mpo", -1)


def both_calls(meta, blocks, low, pair, turned, envs, others):
    blocks, pair = lax.optimization_barrier((blocks, pair))
    whole = sent(blocks, GROUPS[0][1:])
    one, back_one, two = first_round(pair)
    one, back_one, two, low = lax.optimization_barrier((one, back_one, two, low))
    part = sent(low, GROUPS[1])
    shares = [back_one, pair, one, two, *second_round(one, back_one, two)]
    total = apply_terms(0, meta, [blocks, *whole], [], (((0,), None), ((1,), None), ((2,), None)), turned, envs)
    return apply_terms(1, meta, part, shares, (((0,), 0), ((1,), 1)), turned, envs, [total, *others])


def local(wavefunction, left_env, right_env, sector_dims, charges, term_class):
    planes = lax.axis_size("mpo")
    sec_dev = wavefunction.shape[0]
    envs = (left_env, right_env)
    masked, low, masked_share, high_share = mask_blocks(sector_dims, wavefunction, planes)
    pair = jnp.stack(sent(high_share, GROUPS[1]))
    meta = make_plan(charges, term_class, sec_dev)
    pieces = both_calls(meta, masked, low, pair, False, envs, [masked])
    sigma, payload = sum_parts(sector_dims, reduce_over_planes(pieces))

    pair, sums = make_pair(*sent(payload, GROUPS[1]))
    one, back_one, two = first_round(sigma)
    some, more = spread(sums)
    full, low = assemble([back_one, sigma, one, two, *second_round(one, back_one, two)])
    full, pair, some, more = lax.optimization_barrier((full, pair, some, more))

    pieces = both_calls(meta, full, low, pair, True, envs, [some + more])
    return finish(sector_dims, reduce_over_planes(pieces), sigma, masked_share)


def solution(mesh):
    placed = (
        P("sec", None, None),
        P("mpo", "sec", None, None),
        P("mpo", "sec", None, None),
        P("sec", None),
        P(),
        P("mpo"),
    )
    return jax.shard_map(
        local,
        mesh=mesh,
        in_specs=placed,
        out_specs=(P("sec", "mpo", None), P("sec", "mpo", None)),
        check_vma=False,
    )
```
